128 devices in a mesh: dp: 8 (over z, x_hi), latent: 16 (over x_lo, y, core).
Axes of the slice: x: 4 (x_hi: 2, x_lo: 2; x = x_hi * 2 + x_lo), y: 4, z: 4, core: 2. Of those that a mesh axis runs over, the one named last changes fastest.
Arguments:
- tokens: bfloat16 [512, 4608], P(('dp', 'latent')), may hold values from -6 to 6
- batch_order: int32 [512], replicated, may hold values from 0 to 511, each once
- enc_weight: bfloat16 [4608, 65536], P(None, ('dp', 'latent')), may hold values from -0.09375 to 0.09375
- enc_bias: float32 [65536], P(('dp', 'latent')), may hold values from -0.5 to 0.5
- dec_weight: bfloat16 [65536, 4608], P(('dp', 'latent')), may hold values from -0.25 to 0.25
Outputs:
- recon_error: float32 [512, 4608], P(('dp', 'latent'))
- enc_grad: bfloat16 [4608, 65536], P(None, ('dp', 'latent'))
- dec_grad: bfloat16 [65536, 4608], P(('dp', 'latent'))
- bias_grad: float32 [65536], P(('dp', 'latent'))
The draws below stay inside these ranges and needn't reach their ends.
Inputs may be any that keep to these rules, and one draw needn't show every extreme that they name: `batch_order`: each number from 0 to 511 appears once.
All inputs are finite; a program needn't handle non-finite values.
Results may differ from the reference program's by a relative error of at most 0.025.
Values may be sent and summed in bfloat16 or wider, within the bound.
No kernel may reach another device: no remote copies, remote signals or barrier semaphores. Data moves between devices by JAX's collectives and lax.ppermute only.
A program may use at most 128 MiB of HBM per device.

```python
import math
import jax
import jax.numpy as jnp
from jax import lax

D = 4608
LATENTS = 65536
ROWS = 512


def draw_dec_weight(key, part):
    keys = jax.random.split(jax.random.fold_in(key, 17), 3)
    column_scale = jnp.exp(jax.random.uniform(keys[0], (D,), jnp.float32, 0.0, math.log(10.0))) / 4.64
    latent_scale = jnp.exp(jax.random.uniform(keys[1], (LATENTS, 1), jnp.float32, -math.log(2.0), math.log(2.0))) / 1.16
    values = jax.random.truncated_normal(keys[2], -4.0, 4.0, (LATENTS, D), jnp.float32)
    scaled = values * latent_scale * column_scale / math.sqrt(2.0 * LATENTS)
    scaled = jnp.clip(scaled, -0.25, 0.25)
    return scaled.astype(jnp.bfloat16)


def block_scale(rng, shape, cuts, smallest, largest):
    gain = 1.0
    for position, parts in cuts:
        draws = jax.random.uniform(jax.random.fold_in(jax.random.fold_in(rng, 6), position), (parts,), jnp.float32, smallest / len(cuts), largest / len(cuts))
        gain = gain * jnp.repeat(jnp.exp(draws), shape[position] // parts).reshape((-1,) + (1,) * (len(shape) - 1 - position))
    return gain


def centred(own_key, dims, scale, most, shards=(), held_as=jnp.bfloat16):
    drawn = jax.random.normal(own_key, dims, jnp.float32) * scale
    if len(shards) > 0:
        drawn = block_scale(own_key, dims, shards, -0.22, 0.18) * drawn
    return jnp.clip(drawn, min=-most, max=most).astype(held_as)


def setup_inputs(seed: int = 0) -> dict:
    key_of = jax.random.split(jax.random.key(seed), 6)
    tokens = centred(key_of[0], (ROWS, D), 1.0, 6.0, ((0, 128),))
    batch_order = jax.random.permutation(key_of[1], ROWS).astype(jnp.int32)
    enc_weight = centred(key_of[2], (D, LATENTS), D ** -0.5, 0.09375, ((1, 128),))
    enc_bias = jnp.clip(jax.random.uniform(key_of[3], (LATENTS,), jnp.float32, -0.5, 0.5) * block_scale(key_of[3], (LATENTS,), ((0, 128),), -0.4, 0.0), -0.5, 0.5)
    dec_weight = draw_dec_weight(jax.random.fold_in(key_of[5], 71), 0)
    return {"tokens": tokens, "batch_order": batch_order, "enc_weight": enc_weight, "enc_bias": enc_bias, "dec_weight": dec_weight}


def reference(tokens, batch_order, enc_weight, enc_bias, dec_weight):
    inputs = jnp.take(tokens, batch_order, axis=0)
    preact = jnp.dot(inputs, enc_weight, preferred_element_type=jnp.float32) + enc_bias
    positive = jnp.maximum(preact, 0.0)
    activations = positive.astype(jnp.bfloat16)
    recon_error = jnp.dot(activations, dec_weight, preferred_element_type=jnp.float32) - inputs.astype(jnp.float32)
    row_scale = math.sqrt(ROWS)
    err_grad = (recon_error / row_scale).astype(jnp.bfloat16)
    dec_wide = dec_weight.astype(jnp.float32)
    row_norms = jnp.sqrt(lax.optimization_barrier(jnp.sum(dec_wide * dec_wide, axis=1)) + 1e-06)
    act_total = lax.optimization_barrier(jnp.sum(activations.astype(jnp.float32), axis=0)) / row_scale
    dec_grad = jnp.dot(activations.T, err_grad, preferred_element_type=jnp.float32)
    dec_grad = (dec_grad + act_total[:, None] * dec_wide / row_norms[:, None]).astype(jnp.bfloat16)
    act_grad = jnp.dot(err_grad, dec_weight.T, preferred_element_type=jnp.float32) + row_norms / row_scale
    pre_grad = jnp.where(preact > 0.0, act_grad, jnp.zeros_like(act_grad)).astype(jnp.bfloat16)
    enc_grad = jnp.dot(inputs.T, pre_grad, preferred_element_type=jnp.float32).astype(jnp.bfloat16)
    bias_grad = lax.optimization_barrier(jnp.sum(pre_grad.astype(jnp.float32), axis=0))
    return (recon_error, enc_grad, dec_grad, bias_grad)
```

```python
import math

import jax
import jax.numpy as jnp
from jax import lax
from jax.sharding import Mesh, PartitionSpec as P

CHIPS = ("z", "xh", "xl", "y")
SWAP = [(0, 1), (1, 0)]


def gather_chips(block):
    chips = lax.axis_size(CHIPS)
    copies = jnp.broadcast_to(block[None], (chips,) + block.shape)
    out = lax.all_to_all(copies, CHIPS, 0, 0)
    return out.reshape(chips * block.shape[0], block.shape[1])


def per_device(tokens, batch_order, enc_weight, enc_bias, dec_weight):
    rows_dev, width = tokens.shape
    total_rows = batch_order.shape[0]
    row_scale = math.sqrt(total_rows)
    half = width // 2
    chips = lax.axis_size(CHIPS)
    contract_rows = (((0,), (0,)), ((), ()))
    core = lax.axis_index("c")
    own = core * half
    oth = (1 - core) * half

    def pick(a, start):
        return lax.dynamic_slice_in_dim(a, start, half, 1)

    got = lax.ppermute(pick(tokens, oth), "c", SWAP)
    mine = pick(tokens, own)
    block = jnp.where(core == 0, jnp.concatenate([mine, got]), jnp.concatenate([got, mine]))
    x_own = gather_chips(block)
    x_oth = lax.ppermute(x_own, "c", SWAP)
    inputs = jnp.where(core == 0, jnp.concatenate([x_own, x_oth], 1), jnp.concatenate([x_oth, x_own], 1))
    preact = jnp.dot(inputs, enc_weight, preferred_element_type=jnp.float32) + enc_bias
    activations = jnp.maximum(preact, 0.0).astype(jnp.bfloat16)

    part_oth = jnp.dot(activations, pick(dec_weight, oth), preferred_element_type=jnp.float32)
    part_got = lax.ppermute(part_oth.astype(jnp.bfloat16), "c", SWAP)
    part_own = jnp.dot(activations, pick(dec_weight, own), preferred_element_type=jnp.float32)
    part = (part_own + part_got.astype(jnp.float32)).astype(jnp.bfloat16)
    pieces = lax.all_to_all(part.reshape(chips, total_rows // chips, half), CHIPS, 0, 0)
    recon = jnp.sum(pieces.astype(jnp.float32), axis=0) - block.astype(jnp.float32)
    err_block = (recon / row_scale).astype(jnp.bfloat16)
    e_own = gather_chips(err_block)
    e_oth = lax.ppermute(e_own, "c", SWAP)
    err = jnp.where(core == 0, jnp.concatenate([e_own, e_oth], 1), jnp.concatenate([e_oth, e_own], 1))

    dec_wide = dec_weight.astype(jnp.float32)
    row_norms = jnp.sqrt(jnp.sum(dec_wide * dec_wide, axis=1) + 1e-06)
    act_total = jnp.sum(activations.astype(jnp.float32), axis=0) / row_scale
    dec_accum = lax.dot_general(activations, err, contract_rows, preferred_element_type=jnp.float32)
    dec_grad = (dec_accum + act_total[:, None] * dec_wide / row_norms[:, None]).astype(jnp.bfloat16)
    act_grad = lax.dot_general(err, dec_weight, (((1,), (1,)), ((), ())), preferred_element_type=jnp.float32)
    act_grad = act_grad + row_norms / row_scale
    pre_grad = jnp.where(preact > 0.0, act_grad, 0.0).astype(jnp.bfloat16)
    enc_grad = lax.dot_general(inputs, pre_grad, contract_rows, preferred_element_type=jnp.float32)
    bias_grad = jnp.sum(pre_grad.astype(jnp.float32), axis=0)

    first = lax.axis_index(CHIPS + ("c",)) * rows_dev
    wanted = lax.dynamic_slice_in_dim(batch_order, first, rows_dev)
    recon_error = jnp.take(err, wanted, axis=0).astype(jnp.float32) * row_scale
    return (recon_error, enc_grad.astype(jnp.bfloat16), dec_grad, bias_grad)


def solution(mesh):
    names = CHIPS + ("c",)
    split = Mesh(mesh.devices.reshape(4, 2, 2, 4, 2), names)
    return jax.shard_map(
        per_device,
        mesh=split,
        in_specs=(P(names, None), P(), P(None, names), P(names), P(names, None)),
        out_specs=(P(names, None), P(None, names), P(names, None), P(names)),
        check_vma=False,
    )
```

```python
import functools
import itertools
import math

import jax
import jax.numpy as jnp
from jax import lax
from jax.experimental import pallas as pl
from jax.experimental.pallas import tpu as pltpu
from jax.sharding import Mesh, PartitionSpec as P

CHIPS = ("z", "xh", "xl", "y")
NAMES = CHIPS + ("c",)
SWAP = [(0, 1), (1, 0)]


def chip_index(z, x, y):
    return ((z % 4) * 4 + x % 4) * 4 + y % 4


def chip_classes():
    groups = []
    for b, a in itertools.product(range(2), range(2)):
        group = []
        for z, x, y in itertools.product(range(4), range(2), range(2)):
            group.append(chip_index(z, 2 * x + (a + z) % 2, 2 * y + (b + z) % 2))
        groups.append(group)
    return groups


def neighbour_shifts():
    shifts = []
    for step in ((0, 1, 0), (0, 0, 1), (1, 0, 0)):
        pairs = []
        for z, x, y in itertools.product(range(4), repeat=3):
            for c in range(2):
                s = 1 - 2 * c
                to = chip_index(z + s * step[0], x + s * step[1], y + s * step[2])
                pairs.append((chip_index(z, x, y) * 2 + c, to * 2 + c))
        shifts.append(pairs)
    return shifts


CLASSES = chip_classes()
SHIFTS = neighbour_shifts()


def gather_chips(block):
    copies = jnp.broadcast_to(block[None], (16,) + block.shape)
    near = lax.all_to_all(copies, CHIPS, 0, 0, axis_index_groups=CLASSES)
    near = near.reshape(16 * block.shape[0], block.shape[1])
    return [near] + [lax.ppermute(near, NAMES, pairs) for pairs in SHIFTS]


def reduce_chips(parts):
    got = [lax.ppermute(part, NAMES, pairs) for part, pairs in zip(parts[1:], SHIFTS)]
    total = parts[0].astype(jnp.float32)
    for part in got:
        total = total + part.astype(jnp.float32)
    total = total.astype(jnp.bfloat16)
    pieces = total.reshape(16, total.shape[0] // 16, total.shape[1])
    pieces = lax.all_to_all(pieces, CHIPS, 0, 0, axis_index_groups=CLASSES)
    return jnp.sum(pieces.astype(jnp.float32), axis=0)


def swap_cores(a):
    return lax.ppermute(a, "c", SWAP)


def column_block(n, step, core):
    return jnp.where(step < n, core * n + step, (1 - core) * n + step - n)


def front_kernel(n, core, bias_ref, enc_ref, *refs):
    x_own, x_oth = refs[:4], refs[4:8]
    preact_ref, act_ref, total = refs[8:]
    step = pl.program_id(0)

    def add(blocks):
        rows = jnp.concatenate([r[...] for r in blocks], axis=0)
        return jnp.dot(rows, enc_ref[...], preferred_element_type=jnp.float32)

    @pl.when(step == 0)
    def _():
        total[...] = add(x_own)

    @pl.when((step > 0) & (step < n))
    def _():
        total[...] += add(x_own)

    @pl.when((step >= n) & (step < 2 * n - 1))
    def _():
        total[...] += add(x_oth)

    @pl.when(step == 2 * n - 1)
    def _():
        preact = total[...] + add(x_oth) + bias_ref[...]
        preact_ref[...] = preact
        act_ref[...] = jnp.maximum(preact, 0.0).astype(jnp.bfloat16)


def front(core, x_own, x_oth, enc_weight, enc_bias, n):
    rows, half = x_own[0].shape
    latents = enc_weight.shape[1]
    total_rows = 4 * rows
    wide = half // n

    def whole(shape):
        return pl.BlockSpec(shape, lambda i, c: (0, 0))

    own = pl.BlockSpec((rows, wide), lambda i, c: (0, jnp.minimum(i, n - 1)))
    oth = pl.BlockSpec((rows, wide), lambda i, c: (0, jnp.maximum(i - n, 0)))
    return pl.pallas_call(
        functools.partial(front_kernel, n),
        out_shape=(
            jax.ShapeDtypeStruct((total_rows, latents), jnp.float32),
            jax.ShapeDtypeStruct((total_rows, latents), jnp.bfloat16),
        ),
        grid_spec=pltpu.PrefetchScalarGridSpec(
            num_scalar_prefetch=1,
            grid=(2 * n,),
            in_specs=[whole((1, latents)), pl.BlockSpec((wide, latents), lambda i, c: (column_block(n, i, c[0]), 0))]
            + [own] * 4
            + [oth] * 4,
            out_specs=(whole((total_rows, latents)), whole((total_rows, latents))),
            scratch_shapes=[pltpu.VMEM((total_rows, latents), jnp.float32)],
        ),
        compiler_params=pltpu.CompilerParams(vmem_limit_bytes=40 * 2**20),
        name="front",
    )(core, enc_bias[None], enc_weight, *x_own, *x_oth)


def tail_kernel(n, row_scale, core, left_ref, preact_ref, scale_ref, norm_ref, dec_ref, *refs):
    e_own, e_oth, x_own, x_oth = refs[:4], refs[4:8], refs[8:12], refs[12:16]
    dec_grad_ref, enc_grad_ref, bias_ref, recon_ref, total, pre = refs[16:]
    step = pl.program_id(0)
    latents = dec_ref.shape[0]
    out_rows = recon_ref.shape[0]

    @pl.when(step == 0)
    def _():
        total[...] = jnp.zeros_like(total)

    def stack(blocks):
        return jnp.concatenate([r[...] for r in blocks], axis=0)

    def first(blocks):
        err = stack(blocks)
        dec = dec_ref[...]
        both = jnp.dot(left_ref[...], err, preferred_element_type=jnp.float32)
        dec_grad_ref[...] = (both[:latents] + scale_ref[...] * dec.astype(jnp.float32)).astype(jnp.bfloat16)
        recon_ref[...] = both[latents : latents + out_rows] * row_scale
        total[...] += lax.dot_general(err, dec, (((1,), (1,)), ((), ())), preferred_element_type=jnp.float32)

    def second(blocks):
        enc_grad_ref[...] = lax.dot_general(
            stack(blocks), pre[...], (((0,), (0,)), ((), ())), preferred_element_type=jnp.float32
        ).astype(jnp.bfloat16)

    @pl.when(step < n)
    def _():
        first(e_own)

    @pl.when((step >= n) & (step < 2 * n))
    def _():
        first(e_oth)

    @pl.when(step == 2 * n)
    def _():
        rounded = jnp.where(preact_ref[...] > 0.0, total[...] + norm_ref[...], 0.0).astype(jnp.bfloat16)
        pre[...] = rounded
        bias_ref[...] = jnp.sum(rounded.astype(jnp.float32), axis=0, keepdims=True)

    @pl.when((step >= 2 * n) & (step < 3 * n))
    def _():
        second(x_own)

    @pl.when(step >= 3 * n)
    def _():
        second(x_oth)


def tail(core, left, preact, scale, norm, dec_weight, e_own, e_oth, x_own, x_oth, row_scale, out_rows, n):
    rows, half = x_own[0].shape
    latents, width = dec_weight.shape
    wide = half // n
    total_rows = 4 * rows

    def whole(shape):
        return pl.BlockSpec(shape, lambda i, c: (0, 0))

    def part(k):
        return pl.BlockSpec((rows, wide), lambda i, c: (0, jnp.clip(i - k * n, 0, n - 1)))

    def columns(height):
        return pl.BlockSpec((height, wide), lambda i, c: (0, column_block(n, jnp.minimum(i, 2 * n - 1), c[0])))

    return pl.pallas_call(
        functools.partial(tail_kernel, n, row_scale),
        out_shape=(
            jax.ShapeDtypeStruct((latents, width), jnp.bfloat16),
            jax.ShapeDtypeStruct((width, latents), jnp.bfloat16),
            jax.ShapeDtypeStruct((1, latents), jnp.float32),
            jax.ShapeDtypeStruct((out_rows, width), jnp.float32),
        ),
        grid_spec=pltpu.PrefetchScalarGridSpec(
            num_scalar_prefetch=1,
            grid=(4 * n,),
            in_specs=[
                whole(left.shape),
                whole(preact.shape),
                whole(scale.shape),
                whole(norm.shape),
                columns(latents),
            ]
            + [part(k) for k in range(4) for _ in range(4)],
            out_specs=(
                columns(latents),
                pl.BlockSpec((wide, latents), lambda i, c: (column_block(n, jnp.maximum(i - 2 * n, 0), c[0]), 0)),
                whole((1, latents)),
                columns(out_rows),
            ),
            scratch_shapes=[
                pltpu.VMEM((total_rows, latents), jnp.float32),
                pltpu.VMEM((total_rows, latents), jnp.bfloat16),
            ],
        ),
        compiler_params=pltpu.CompilerParams(vmem_limit_bytes=48 * 2**20),
        name="tail",
    )(core, left, preact, scale, norm, dec_weight, *e_own, *e_oth, *x_own, *x_oth)


def per_device(tokens, batch_order, enc_weight, enc_bias, dec_weight):
    rows_dev, width = tokens.shape
    total_rows = batch_order.shape[0]
    row_scale = math.sqrt(total_rows)
    half = width // 2
    block_rows = total_rows // 4
    core = lax.axis_index("c")
    core_arg = core[None].astype(jnp.int32)
    own = core * half
    oth = (1 - core) * half

    def pick(a, start):
        return lax.dynamic_slice_in_dim(a, start, half, 1)

    got = swap_cores(pick(tokens, oth))
    mine = pick(tokens, own)
    block = jnp.where(core == 0, jnp.concatenate([mine, got]), jnp.concatenate([got, mine]))
    x_own = gather_chips(block)
    x_oth = [swap_cores(a) for a in x_own]
    preact, activations = front(core_arg, x_own, x_oth, enc_weight, enc_bias, 3)

    part_oth = jnp.dot(activations, pick(dec_weight, oth), preferred_element_type=jnp.float32).astype(jnp.bfloat16)
    part_own = jnp.dot(activations, pick(dec_weight, own), preferred_element_type=jnp.float32)
    parts = []
    for k in range(4):
        rows = slice(k * block_rows, (k + 1) * block_rows)
        parts.append((part_own[rows] + swap_cores(part_oth[rows]).astype(jnp.float32)).astype(jnp.bfloat16))

    dec_wide = dec_weight.astype(jnp.float32)
    row_norms = jnp.sqrt(jnp.sum(dec_wide * dec_wide, axis=1) + 1e-06)
    act_total = jnp.sum(activations.astype(jnp.float32), axis=0) / row_scale
    z = lax.axis_index("z")
    x = lax.axis_index("xh") * 2 + lax.axis_index("xl")
    y = lax.axis_index("y")
    first = (chip_index(z, x, y) * 2 + core) * rows_dev
    wanted = lax.dynamic_slice_in_dim(batch_order, first, rows_dev)
    chip = wanted // (2 * rows_dev)
    tz, tx, ty = chip // 16, chip // 4 % 4, chip % 4
    a = (tx + tz + x + z) % 2
    b = (ty + tz + y + z) % 2
    place = (a + 2 * b) * block_rows + (tz * 4 + tx // 2 * 2 + ty // 2) * (2 * rows_dev) + wanted % (2 * rows_dev)
    place = jnp.concatenate([place, jnp.full((16 - rows_dev,), -1, place.dtype)])
    chosen = (place[:, None] == jnp.arange(total_rows, dtype=place.dtype)[None]).astype(jnp.bfloat16)
    left = jnp.concatenate([activations.T, chosen])
    scale = (act_total / row_norms)[:, None]
    norm = (row_norms / row_scale)[None]

    recon = reduce_chips(parts) - block.astype(jnp.float32)
    recon, left, scale, norm = lax.optimization_barrier((recon, left, scale, norm))
    err_block = (recon / row_scale).astype(jnp.bfloat16)
    e_own = gather_chips(err_block)
    e_oth = [swap_cores(a) for a in e_own]
    dec_grad, enc_grad, bias_grad, recon_error = tail(
        core_arg, left, preact, scale, norm, dec_weight, e_own, e_oth, x_own, x_oth, row_scale, rows_dev, 3
    )
    return (recon_error, enc_grad, dec_grad, bias_grad[0])


def solution(mesh):
    split = Mesh(mesh.devices.reshape(4, 2, 2, 4, 2), NAMES)
    return jax.shard_map(
        per_device,
        mesh=split,
        in_specs=(P(NAMES, None), P(), P(None, NAMES), P(NAMES), P(NAMES, None)),
        out_specs=(P(NAMES, None), P(None, NAMES), P(NAMES, None), P(NAMES)),
        check_vma=False,
    )
```

```python
import functools
import itertools
import math

import jax
import jax.numpy as jnp
from jax import lax
from jax.experimental import pallas as pl
from jax.experimental.pallas import tpu as pltpu
from jax.sharding import Mesh, PartitionSpec as P

CHIPS = ("z", "xh", "xl", "y")
NAMES = CHIPS + ("c",)
SWAP = [(0, 1), (1, 0)]
SMALL_VMEM = 12 * 2**20
TAIL_VMEM = 20 * 2**20
SMEM = pl.BlockSpec(memory_space=pltpu.SMEM)
VMEM = pl.BlockSpec(memory_space=pltpu.VMEM)
ANY = pl.BlockSpec(memory_space=pl.ANY)
HBM = pl.BlockSpec(memory_space=pltpu.HBM)


def chip_index(z, x, y):
    return ((z % 4) * 4 + x % 4) * 4 + y % 4


def chip_classes():
    groups = []
    for b, a in itertools.product(range(2), range(2)):
        group = []
        for z, x, y in itertools.product(range(4), range(2), range(2)):
            group.append(chip_index(z, 2 * x + (a + z) % 2, 2 * y + (b + z) % 2))
        groups.append(group)
    return groups


def neighbour_shifts():
    shifts = []
    for step in ((0, 1, 0), (0, 0, 1), (1, 0, 0)):
        pairs = []
        for z, x, y in itertools.product(range(4), repeat=3):
            for c in range(2):
                s = 1 - 2 * c
                to = chip_index(z + s * step[0], x + s * step[1], y + s * step[2])
                pairs.append((chip_index(z, x, y) * 2 + c, to * 2 + c))
        shifts.append(pairs)
    return shifts


CLASSES = chip_classes()
SHIFTS = neighbour_shifts()


def gather_chips(block):
    copies = jnp.broadcast_to(block[None], (16,) + block.shape)
    near = lax.all_to_all(copies, CHIPS, 0, 0, axis_index_groups=CLASSES)
    near = near.reshape(16 * block.shape[0], block.shape[1])
    return [near] + [lax.ppermute(near, NAMES, pairs) for pairs in SHIFTS]


def swap_cores(a):
    return lax.ppermute(a, "c", SWAP)


def stack(blocks):
    return jnp.concatenate([ref[...] for ref in blocks], axis=0)


def estimate(flops, moved):
    return pl.CostEstimate(flops=flops, bytes_accessed=moved, transcendentals=0)


def load_kernel(core_ref, near_ref, enc_ref, dec_ref, enc_own, enc_oth, dec_own, dec_oth, sems):
    half = enc_own.shape[0]
    copies = []
    for k, (enc, dec) in enumerate(((enc_own, dec_own), (enc_oth, dec_oth))):
        base = pl.multiple_of(jnp.where(core_ref[0] == k, 0, half), 128)
        copies.append(pltpu.make_async_copy(enc_ref.at[pl.ds(base, half), :], enc, sems.at[k, 0]))
        copies.append(pltpu.make_async_copy(dec_ref.at[:, pl.ds(base, half)], dec, sems.at[k, 1]))
    for copy in copies:
        copy.start()
    for copy in copies:
        copy.wait()


def load(core, near, enc_weight, dec_weight):
    width, latents = enc_weight.shape
    half = width // 2
    enc_half = jax.ShapeDtypeStruct((half, latents), jnp.bfloat16)
    dec_half = jax.ShapeDtypeStruct((latents, half), jnp.bfloat16)
    return pl.pallas_call(
        load_kernel,
        out_shape=(enc_half, enc_half, dec_half, dec_half),
        in_specs=[SMEM, ANY, HBM, HBM],
        out_specs=(VMEM,) * 4,
        scratch_shapes=[pltpu.SemaphoreType.DMA((2, 2))],
        compiler_params=pltpu.CompilerParams(vmem_limit_bytes=SMALL_VMEM),
        cost_estimate=estimate(0, 8 * width * latents),
        name="load",
    )(core, near, enc_weight, dec_weight)


def pre_kernel(enc_ref, x0, x1, x2, x3, total_ref):
    total_ref[...] = jnp.dot(stack((x0, x1, x2, x3)), enc_ref[...], preferred_element_type=jnp.float32)


def pre(x_own, enc_own):
    rows, half = x_own[0].shape
    latents = enc_own.shape[1]
    return pl.pallas_call(
        pre_kernel,
        out_shape=jax.ShapeDtypeStruct((4 * rows, latents), jnp.float32),
        in_specs=[VMEM] * 5,
        out_specs=VMEM,
        compiler_params=pltpu.CompilerParams(vmem_limit_bytes=SMALL_VMEM),
        cost_estimate=estimate(8 * rows * half * latents, 4 * rows * half),
        name="pre",
    )(enc_own, *x_own)


def front_kernel(n, bias_ref, total_ref, enc_ref, dec_ref, x0, x1, x2, x3, preact_ref, act_ref, *part_refs):
    rows, half = x0.shape
    wide = half // n
    product = jnp.dot(stack((x0, x1, x2, x3)), enc_ref[...], preferred_element_type=jnp.float32)
    preact = total_ref[...] + product + bias_ref[...]
    preact_ref[...] = preact
    act_ref[...] = jnp.maximum(preact, 0.0).astype(jnp.bfloat16)
    for k in range(n):
        cols = slice(k * wide, (k + 1) * wide)
        product = jnp.dot(act_ref[...], dec_ref[:, cols], preferred_element_type=jnp.float32).astype(jnp.bfloat16)
        for b, ref in enumerate(part_refs):
            ref[:, cols] = product[b * rows : (b + 1) * rows]


def front(total, x_oth, enc_oth, enc_bias, dec_oth, n):
    rows, half = x_oth[0].shape
    total_rows, latents = total.shape
    out = pl.pallas_call(
        functools.partial(front_kernel, n),
        out_shape=[
            jax.ShapeDtypeStruct((total_rows, latents), jnp.float32),
            jax.ShapeDtypeStruct((total_rows, latents), jnp.bfloat16),
        ]
        + [jax.ShapeDtypeStruct((rows, half), jnp.bfloat16)] * 4,
        in_specs=[VMEM] * 8,
        out_specs=[VMEM] * 6,
        compiler_params=pltpu.CompilerParams(vmem_limit_bytes=SMALL_VMEM),
        cost_estimate=estimate(4 * total_rows * latents * half, 8 * latents * half),
        name="front",
    )(enc_bias[None], total, enc_oth, dec_oth, *x_oth)
    return out[0], out[1], out[2:]


def own_kernel(n, act_ref, dec_ref, *part_refs):
    rows, half = part_refs[0].shape
    wide = half // n
    for k in range(n):
        cols = slice(k * wide, (k + 1) * wide)
        product = jnp.dot(act_ref[...], dec_ref[:, cols], preferred_element_type=jnp.float32).astype(jnp.bfloat16)
        for b, ref in enumerate(part_refs):
            ref[:, cols] = product[b * rows : (b + 1) * rows]


def own_parts(act, dec_own, n):
    total_rows, latents = act.shape
    half = dec_own.shape[1]
    return pl.pallas_call(
        functools.partial(own_kernel, n),
        out_shape=[jax.ShapeDtypeStruct((total_rows // 4, half), jnp.bfloat16)] * 4,
        in_specs=[VMEM] * 2,
        out_specs=[VMEM] * 4,
        compiler_params=pltpu.CompilerParams(vmem_limit_bytes=SMALL_VMEM),
        cost_estimate=estimate(2 * total_rows * latents * half, 6 * latents * half),
        name="own_parts",
    )(act, dec_own)


def side_kernel(row_scale, place_ref, act_ref, dec_own, dec_oth, left_ref, scale_ref, norm_ref):
    latents, half = dec_own.shape
    total_rows = act_ref.shape[0]
    act = act_ref[...]
    left_ref[:latents] = act.T
    spot = lax.broadcasted_iota(jnp.int32, (16, total_rows), 0)
    target = jnp.full((16, total_rows), -1, jnp.int32)
    for r in range(place_ref.shape[0]):
        target = jnp.where(spot == r, place_ref[r], target)
    chosen = lax.broadcasted_iota(jnp.int32, (16, total_rows), 1) == target
    left_ref[latents:] = jnp.where(chosen, 1.0, 0.0).astype(jnp.bfloat16)
    total = jnp.sum(act.astype(jnp.float32), axis=0, keepdims=True) / row_scale
    total = jnp.broadcast_to(total, (128, latents)).T[:, :1]
    squares = jnp.zeros((latents, 128), jnp.float32)
    for dec in (dec_own, dec_oth):
        for c in range(half // 128):
            wide = dec[:, c * 128 : (c + 1) * 128].astype(jnp.float32)
            squares = squares + wide * wide
    norms = jnp.sqrt(jnp.sum(squares, axis=1, keepdims=True) + 1e-06)
    scale_ref[...] = total / norms
    norm_ref[...] = jnp.broadcast_to(norms / row_scale, (latents, 128)).T[:1]


def side(place, act, dec_own, dec_oth, row_scale):
    total_rows, latents = act.shape
    width = 2 * dec_own.shape[1]
    return pl.pallas_call(
        functools.partial(side_kernel, row_scale),
        out_shape=(
            jax.ShapeDtypeStruct((latents + 16, total_rows), jnp.bfloat16),
            jax.ShapeDtypeStruct((latents, 1), jnp.float32),
            jax.ShapeDtypeStruct((1, latents), jnp.float32),
        ),
        in_specs=[SMEM] + [VMEM] * 3,
        out_specs=(VMEM, VMEM, VMEM),
        compiler_params=pltpu.CompilerParams(vmem_limit_bytes=SMALL_VMEM),
        cost_estimate=estimate(4 * latents * width, 2 * latents * width),
        name="side",
    )(place, act, dec_own, dec_oth)


def decoder_half(n, base, row_scale, left_ref, scale_ref, dec_ref, err, dec_out, dec_grad_ref, recon_ref, sems):
    latents, half = dec_ref.shape
    wide = half // n
    outs = []
    for k in range(n):
        cols = slice(k * wide, (k + 1) * wide)
        both = jnp.dot(left_ref[...], err[:, cols], preferred_element_type=jnp.float32)
        grad = both[:latents] + scale_ref[...] * dec_ref[:, cols].astype(jnp.float32)
        dec_out[k] = grad.astype(jnp.bfloat16)
        start = pl.multiple_of(base + k * wide, 128)
        out = pltpu.make_async_copy(dec_out.at[k], dec_grad_ref.at[:, pl.ds(start, wide)], sems.at[k])
        out.start()
        outs.append(out)
        recon_ref[k] = both[latents : latents + recon_ref.shape[1]] * row_scale
    return outs


def grad_own_kernel(n, row_scale, core_ref, left_ref, scale_ref, dec_ref, *refs):
    blocks = refs[:4]
    total_ref, recon_ref, dec_grad_ref, dec_out, sems = refs[4:]
    half = dec_ref.shape[1]
    err = stack(blocks)
    outs = decoder_half(
        n, core_ref[0] * half, row_scale, left_ref, scale_ref, dec_ref, err, dec_out, dec_grad_ref, recon_ref, sems
    )
    total_ref[...] = lax.dot_general(err, dec_ref[...], (((1,), (1,)), ((), ())), preferred_element_type=jnp.float32)
    for out in outs:
        out.wait()


def grad_own(core, left, scale, dec_own, e_own, row_scale, out_rows, n):
    rows, half = e_own[0].shape
    latents = dec_own.shape[0]
    wide = half // n
    return pl.pallas_call(
        functools.partial(grad_own_kernel, n, row_scale),
        out_shape=(
            jax.ShapeDtypeStruct((4 * rows, latents), jnp.float32),
            jax.ShapeDtypeStruct((n, out_rows, wide), jnp.float32),
            jax.ShapeDtypeStruct((latents, 2 * half), jnp.bfloat16),
        ),
        in_specs=[SMEM] + [VMEM] * 7,
        out_specs=(VMEM, VMEM, HBM),
        scratch_shapes=[pltpu.VMEM((n, latents, wide), jnp.bfloat16), pltpu.SemaphoreType.DMA((n,))],
        compiler_params=pltpu.CompilerParams(vmem_limit_bytes=SMALL_VMEM),
        cost_estimate=estimate(16 * rows * latents * half, 4 * latents * half),
        name="grad_own",
    )(core, left, scale, dec_own, *e_own)


def tail_kernel(n, row_scale, core_ref, left_ref, preact_ref, scale_ref, norm_ref, total_ref, recon_own, dec_ref, *refs):
    e_oth, x_blocks = refs[:4], (refs[4:8], refs[8:12])
    dec_grad_ref, enc_grad_ref, bias_ref, recon_ref = refs[13:17]
    dec_out, enc_out, recon_oth, pre_ref, dec_sems, enc_sems = refs[17:]
    core = core_ref[0]
    half = dec_ref.shape[1]
    wide = half // n
    bases = (core * half, (1 - core) * half)
    err = stack(e_oth)
    outs = decoder_half(
        n, bases[1], row_scale, left_ref, scale_ref, dec_ref, err, dec_out, dec_grad_ref, recon_oth, dec_sems
    )
    for side_index, held in enumerate((recon_own, recon_oth)):
        for k in range(n):
            recon_ref[:, pl.ds(pl.multiple_of(bases[side_index] + k * wide, 128), wide)] = held[k]
    product = lax.dot_general(err, dec_ref[...], (((1,), (1,)), ((), ())), preferred_element_type=jnp.float32)
    act_grad = total_ref[...] + product + norm_ref[...]
    rounded = jnp.where(preact_ref[...] > 0.0, act_grad, 0.0).astype(jnp.bfloat16)
    pre_ref[...] = rounded
    bias_ref[...] = jnp.sum(rounded.astype(jnp.float32), axis=0, keepdims=True)
    for side_index in range(2):
        for k in range(n):
            spot = side_index * n + k
            mine = jnp.concatenate([ref[:, k * wide : (k + 1) * wide] for ref in x_blocks[side_index]], axis=0)
            grad = lax.dot_general(mine, pre_ref[...], (((0,), (0,)), ((), ())), preferred_element_type=jnp.float32)
            enc_out[spot] = grad.astype(jnp.bfloat16)
            start = pl.multiple_of(bases[side_index] + k * wide, 128)
            out = pltpu.make_async_copy(enc_out.at[spot], enc_grad_ref.at[pl.ds(start, wide), :], enc_sems.at[spot])
            out.start()
            outs.append(out)
    for out in outs:
        out.wait()


def tail(core, left, preact, scale, norm, total, recon_own, dec_oth, e_oth, x_own, x_oth, dec_grad, row_scale, n):
    rows, half = x_own[0].shape
    latents = dec_oth.shape[0]
    width = 2 * half
    wide = half // n
    total_rows = 4 * rows
    out_rows = recon_own.shape[1]
    return pl.pallas_call(
        functools.partial(tail_kernel, n, row_scale),
        out_shape=(
            jax.ShapeDtypeStruct((latents, width), jnp.bfloat16),
            jax.ShapeDtypeStruct((width, latents), jnp.bfloat16),
            jax.ShapeDtypeStruct((1, latents), jnp.float32),
            jax.ShapeDtypeStruct((out_rows, width), jnp.float32),
        ),
        in_specs=[SMEM] + [VMEM] * 19 + [HBM],
        out_specs=(HBM, HBM, VMEM, VMEM),
        scratch_shapes=[
            pltpu.VMEM((n, latents, wide), jnp.bfloat16),
            pltpu.VMEM((2 * n, wide, latents), jnp.bfloat16),
            pltpu.VMEM((n, out_rows, wide), jnp.float32),
            pltpu.VMEM((total_rows, latents), jnp.bfloat16),
            pltpu.SemaphoreType.DMA((n,)),
            pltpu.SemaphoreType.DMA((2 * n,)),
        ],
        input_output_aliases={20: 0},
        compiler_params=pltpu.CompilerParams(vmem_limit_bytes=TAIL_VMEM),
        cost_estimate=estimate(32 * rows * latents * half, 8 * latents * half),
        name="tail",
    )(core, left, preact, scale, norm, total, recon_own, dec_oth, *e_oth, *x_own, *x_oth, dec_grad)


def per_device(tokens, batch_order, enc_weight, enc_bias, dec_weight):
    rows_dev, width = tokens.shape
    total_rows = batch_order.shape[0]
    row_scale = math.sqrt(total_rows)
    half = width // 2
    block_rows = total_rows // 4
    core = lax.axis_index("c")
    core_arg = core[None].astype(jnp.int32)

    z = lax.axis_index("z")
    x = lax.axis_index("xh") * 2 + lax.axis_index("xl")
    y = lax.axis_index("y")
    first = (chip_index(z, x, y) * 2 + core) * rows_dev
    wanted = lax.dynamic_slice_in_dim(batch_order, first, rows_dev)
    chip = wanted // (2 * rows_dev)
    tz, tx, ty = chip // 16, chip // 4 % 4, chip % 4
    a = (tx + tz + x + z) % 2
    b = (ty + tz + y + z) % 2
    place = (a + 2 * b) * block_rows + (tz * 4 + tx // 2 * 2 + ty // 2) * (2 * rows_dev) + wanted % (2 * rows_dev)

    def pick(a, start):
        return lax.dynamic_slice_in_dim(a, start, half, 1)

    got = swap_cores(pick(tokens, (1 - core) * half))
    mine = pick(tokens, core * half)
    block = jnp.where(core == 0, jnp.concatenate([mine, got]), jnp.concatenate([got, mine]))
    block, place = lax.optimization_barrier((block, place))
    x_own = gather_chips(block)
    halves = load(core_arg, x_own[0], enc_weight, dec_weight)
    x_own[1:], halves = lax.optimization_barrier((x_own[1:], halves))
    enc_own, enc_oth, dec_own, dec_oth = halves
    x_oth = [swap_cores(a) for a in x_own]
    partial = pre(x_own, enc_own)
    preact, activations, part_oth = front(partial, x_oth, enc_oth, enc_bias, dec_oth, 3)

    part_got = [swap_cores(part_oth[k]) for k in (1, 2, 3, 0)]
    part_own = own_parts(activations, dec_own, 3)
    sent = [(part_own[k + 1].astype(jnp.float32) + part_got[k].astype(jnp.float32)).astype(jnp.bfloat16) for k in range(3)]
    got = [lax.ppermute(part, NAMES, pairs) for part, pairs in zip(sent, SHIFTS)]
    left, scale, norm = side(place, activations, dec_own, dec_oth, row_scale)
    total = part_own[0].astype(jnp.float32) + part_got[3].astype(jnp.float32)
    for part in got:
        total = total + part.astype(jnp.float32)
    total = total.astype(jnp.bfloat16).reshape(16, block_rows // 16, half)
    total, left, scale, norm = lax.optimization_barrier((total, left, scale, norm))
    pieces = lax.all_to_all(total, CHIPS, 0, 0, axis_index_groups=CLASSES)
    recon = jnp.sum(pieces.astype(jnp.float32), axis=0) - block.astype(jnp.float32)
    err_block = (recon / row_scale).astype(jnp.bfloat16)
    e_own = gather_chips(err_block)
    e_oth = [swap_cores(a) for a in e_own]
    act_part, recon_own, dec_grad = grad_own(core_arg, left, scale, dec_own, e_own, row_scale, rows_dev, 3)
    dec_grad, enc_grad, bias_grad, recon_error = tail(
        core_arg, left, preact, scale, norm, act_part, recon_own, dec_oth, e_oth, x_own, x_oth, dec_grad, row_scale, 3
    )
    return (recon_error, enc_grad, dec_grad, bias_grad[0])


def solution(mesh):
    split = Mesh(mesh.devices.reshape(4, 2, 2, 4, 2), NAMES)
    return jax.shard_map(
        per_device,
        mesh=split,
        in_specs=(P(NAMES, None), P(), P(None, NAMES), P(NAMES), P(NAMES, None)),
        out_specs=(P(NAMES, None), P(None, NAMES), P(NAMES, None), P(NAMES)),
        check_vma=False,
    )
```

```python
import functools
import itertools
import math

import jax
import jax.numpy as jnp
from jax import lax
from jax.experimental import pallas as pl
from jax.experimental.pallas import tpu as pltpu
from jax.sharding import Mesh, PartitionSpec as P

CHIPS = ("z", "xh", "xl", "y")
NAMES = CHIPS + ("c",)
SWAP = [(0, 1), (1, 0)]
SMALL_VMEM = 12 * 2**20
TAIL_VMEM = 20 * 2**20
SMEM = pl.BlockSpec(memory_space=pltpu.SMEM)
VMEM = pl.BlockSpec(memory_space=pltpu.VMEM)
ANY = pl.BlockSpec(memory_space=pl.ANY)
HBM = pl.BlockSpec(memory_space=pltpu.HBM)


def chip_index(z, x, y):
    return ((z % 4) * 4 + x % 4) * 4 + y % 4


def chip_classes():
    groups = []
    for b, a in itertools.product(range(2), range(2)):
        group = []
        for z, x, y in itertools.product(range(4), range(2), range(2)):
            group.append(chip_index(z, 2 * x + (a + z) % 2, 2 * y + (b + z) % 2))
        groups.append(group)
    return groups


def neighbour_shifts():
    shifts = []
    for step in ((0, 1, 0), (0, 0, 1), (1, 0, 0)):
        pairs = []
        for z, x, y in itertools.product(range(4), repeat=3):
            for c in range(2):
                s = 1 - 2 * c
                to = chip_index(z + s * step[0], x + s * step[1], y + s * step[2])
                pairs.append((chip_index(z, x, y) * 2 + c, to * 2 + c))
        shifts.append(pairs)
    return shifts


CLASSES = chip_classes()
SHIFTS = neighbour_shifts()
GROUPS = ((0,), (1,), (2,), (3,))


def near_copies(block):
    copies = jnp.broadcast_to(block[None], (16,) + block.shape)
    near = lax.all_to_all(copies, CHIPS, 0, 0, axis_index_groups=CLASSES)
    return near.reshape(16 * block.shape[0], block.shape[1])


def spread(near):
    return [near] + [lax.ppermute(near, NAMES, pairs) for pairs in SHIFTS]


def swap_cores(a):
    return lax.ppermute(a, "c", SWAP)


def stack(blocks):
    return jnp.concatenate([ref[...] for ref in blocks], axis=0)


def estimate(flops, moved):
    return pl.CostEstimate(flops=flops, bytes_accessed=moved, transcendentals=0)


def params(limit):
    return pltpu.CompilerParams(vmem_limit_bytes=limit)


def chunks(width):
    found, at = [], 0
    while at < width:
        step = min(768, width - at)
        if width - at == 1024:
            step = 512
        found.append((at, step))
        at += step
    return found


def load_kernel(widths, core_ref, near_ref, enc_ref, dec_ref, *refs):
    pieces = 2 * len(widths)
    enc_refs, dec_refs, sems = refs[:pieces], refs[pieces : 2 * pieces], refs[2 * pieces]
    half = sum(widths)
    copies = []
    for k in range(pieces):
        side_index, q = divmod(k, len(widths))
        base = jnp.where(core_ref[0] == side_index, 0, half) + sum(widths[:q])
        base = pl.multiple_of(base, 128)
        cut = pl.ds(base, widths[q])
        copies.append(pltpu.make_async_copy(enc_ref.at[cut, :], enc_refs[k], sems.at[k, 0]))
        copies.append(pltpu.make_async_copy(dec_ref.at[:, cut], dec_refs[k], sems.at[k, 1]))
    for copy in copies:
        copy.start()
    for copy in copies:
        copy.wait()


def load(core, near, enc_weight, dec_weight, widths):
    width, latents = enc_weight.shape
    both = list(widths) * 2
    out = pl.pallas_call(
        functools.partial(load_kernel, widths),
        out_shape=[jax.ShapeDtypeStruct((w, latents), jnp.bfloat16) for w in both]
        + [jax.ShapeDtypeStruct((latents, w), jnp.bfloat16) for w in both],
        in_specs=[SMEM, ANY, HBM, HBM],
        out_specs=[VMEM] * (2 * len(both)),
        scratch_shapes=[pltpu.SemaphoreType.DMA((len(both), 2))],
        compiler_params=params(SMALL_VMEM),
        cost_estimate=estimate(0, 8 * width * latents),
        name="load",
    )(core, near, enc_weight, dec_weight)
    return out[: len(both)], out[len(both) :]


def pipelined(tasks):
    held = None
    for product, use in tasks:
        result = product()
        if held is not None:
            held[0](held[1])
        held = (use, result)
    held[0](held[1])


def part_tasks(act_ref, dec_ref, part_refs):
    rows = part_refs[0].shape[0]

    def task(cols):
        def product():
            return jnp.dot(act_ref[...], dec_ref[:, cols], preferred_element_type=jnp.float32)

        def use(result):
            result = result.astype(jnp.bfloat16)
            for b, ref in enumerate(part_refs):
                ref[:, cols] = result[b * rows : (b + 1) * rows]

        return product, use

    return [task(slice(at, at + step)) for at, step in chunks(dec_ref.shape[1])]


def front_kernel(count, bias_ref, enc_own, enc_oth, dec_ref, *refs):
    x_own, x_oth = refs[:count], refs[count : 2 * count]
    preact_ref, act_ref = refs[2 * count : 2 * count + 2]
    preact = jnp.dot(stack(x_own), enc_own[...], preferred_element_type=jnp.float32)
    preact = preact + jnp.dot(stack(x_oth), enc_oth[...], preferred_element_type=jnp.float32) + bias_ref[...]
    preact_ref[...] = preact
    act_ref[...] = jnp.maximum(preact, 0.0).astype(jnp.bfloat16)
    pipelined(part_tasks(act_ref, dec_ref, refs[2 * count + 2 :]))


def front(x_own, x_oth, encs, enc_bias, dec):
    count = len(x_own)
    rows, half = x_own[0].shape
    latents = dec.shape[0]
    out = pl.pallas_call(
        functools.partial(front_kernel, count),
        out_shape=[
            jax.ShapeDtypeStruct((count * rows, latents), jnp.float32),
            jax.ShapeDtypeStruct((count * rows, latents), jnp.bfloat16),
        ]
        + [jax.ShapeDtypeStruct((rows, half), jnp.bfloat16)] * count,
        in_specs=[VMEM] * (4 + 2 * count),
        out_specs=[VMEM] * (2 + count),
        compiler_params=params(SMALL_VMEM),
        cost_estimate=estimate(6 * count * rows * latents * half, 8 * latents * half),
        name="front",
    )(enc_bias[None], *encs, dec, *x_own, *x_oth)
    return out[0], out[1], out[2:]


def parts_kernel(act_ref, dec_ref, *part_refs):
    pipelined(part_tasks(act_ref, dec_ref, part_refs))


def parts(act, dec, count):
    total_rows, latents = act.shape
    wide = dec.shape[1]
    return pl.pallas_call(
        parts_kernel,
        out_shape=[jax.ShapeDtypeStruct((total_rows // count, wide), jnp.bfloat16)] * count,
        in_specs=[VMEM] * 2,
        out_specs=[VMEM] * count,
        compiler_params=params(SMALL_VMEM),
        cost_estimate=estimate(2 * total_rows * latents * wide, 4 * latents * wide),
        name="parts",
    )(act, dec)


def side_kernel(row_scale, rows_dev, groups, order_ref, *refs):
    acts, decs, (left_ref, scale_ref, norm_ref) = refs[:groups], refs[groups:-3], refs[-3:]
    act = stack(acts)
    total_rows, latents = act.shape
    left_ref[:latents] = act.T
    spot = lax.broadcasted_iota(jnp.int32, (16, total_rows), 0)
    target = jnp.full((16, total_rows), -1, jnp.int32)
    z = lax.axis_index("z")
    x = lax.axis_index("xh") * 2 + lax.axis_index("xl")
    y = lax.axis_index("y")
    first = (((z * 4 + x) * 4 + y) * 2 + lax.axis_index("c")) * rows_dev
    chip_rows = 2 * rows_dev
    for r in range(rows_dev):
        wanted = order_ref[first + r]
        chip = wanted // chip_rows
        tz, tx, ty = chip // 16, chip // 4 % 4, chip % 4
        kind = (tx + tz + x + z) % 2 + 2 * ((ty + tz + y + z) % 2)
        place = (kind * 16 + tz * 4 + tx // 2 * 2 + ty // 2) * chip_rows + wanted % chip_rows
        target = jnp.where(spot == r, place, target)
    chosen = lax.broadcasted_iota(jnp.int32, (16, total_rows), 1) == target
    left_ref[latents:] = jnp.where(chosen, 1.0, 0.0).astype(jnp.bfloat16)
    total = jnp.sum(act.astype(jnp.float32), axis=0, keepdims=True) / row_scale
    total = jnp.broadcast_to(total, (128, latents)).T[:, :1]
    squares = jnp.zeros((latents, 128), jnp.float32)
    for dec in decs:
        for c in range(dec.shape[1] // 128):
            wide = dec[:, c * 128 : (c + 1) * 128].astype(jnp.float32)
            squares = squares + wide * wide
    norms = jnp.sqrt(jnp.sum(squares, axis=1, keepdims=True) + 1e-06)
    scale_ref[...] = total / norms
    norm_ref[...] = jnp.broadcast_to(norms / row_scale, (latents, 128)).T[:1]


def side(order, acts, decs, row_scale, rows_dev):
    total_rows, latents = sum(act.shape[0] for act in acts), acts[0].shape[1]
    width = sum(dec.shape[1] for dec in decs)
    return pl.pallas_call(
        functools.partial(side_kernel, row_scale, rows_dev, len(acts)),
        out_shape=(
            jax.ShapeDtypeStruct((latents + 16, total_rows), jnp.bfloat16),
            jax.ShapeDtypeStruct((latents, 1), jnp.float32),
            jax.ShapeDtypeStruct((1, latents), jnp.float32),
        ),
        in_specs=[SMEM] + [VMEM] * (len(acts) + len(decs)),
        out_specs=(VMEM, VMEM, VMEM),
        compiler_params=params(SMALL_VMEM),
        cost_estimate=estimate(4 * latents * width, 2 * latents * width),
        name="side",
    )(order, *acts, *decs)


def decoder_tasks(base, row_scale, left_ref, scale_ref, dec_ref, err, dec_out, dec_grad_ref, recon_ref, sems, outs):
    latents, wide = dec_ref.shape

    def task(spot, at, step):
        cols = slice(at, at + step)

        def product():
            return jnp.dot(left_ref[...], err[:, cols], preferred_element_type=jnp.float32)

        def use(both):
            grad = both[:latents] + scale_ref[...] * dec_ref[:, cols].astype(jnp.float32)
            dec_out[:, cols] = grad.astype(jnp.bfloat16)
            recon_ref[:, cols] = both[latents : latents + recon_ref.shape[0]] * row_scale
            start = pl.multiple_of(base + at, 128)
            out = pltpu.make_async_copy(dec_out.at[:, cols], dec_grad_ref.at[:, pl.ds(start, step)], sems.at[spot])
            out.start()
            outs.append(out)

        return product, use

    return [task(spot, at, step) for spot, (at, step) in enumerate(chunks(wide))]


def piece_base(core, half, side_index, offset):
    return jnp.where(core == side_index, 0, half) + offset


def grad_kernel(later, side_index, offset, half, row_scale, core_ref, left_ref, scale_ref, dec_ref, *refs):
    blocks, refs = refs[:4], refs[4:]
    before, refs = (refs[0], refs[2:]) if later else (None, refs)
    total_ref, recon_ref, dec_grad_ref, dec_out, sems = refs
    base = piece_base(core_ref[0], half, side_index, offset)
    err = stack(blocks)
    outs = []

    def product():
        return lax.dot_general(err, dec_ref[...], (((1,), (1,)), ((), ())), preferred_element_type=jnp.float32)

    def use(result):
        total_ref[...] = before[...] + result if later else result

    pipelined(
        decoder_tasks(base, row_scale, left_ref, scale_ref, dec_ref, err, dec_out, dec_grad_ref, recon_ref, sems, outs)
        + [(product, use)]
    )
    for out in outs:
        out.wait()


def grad(core, left, scale, dec, blocks, held, side_index, offset, half, row_scale, out_rows):
    rows, wide = blocks[0].shape
    latents = dec.shape[0]
    later = held is not None
    return pl.pallas_call(
        functools.partial(grad_kernel, later, side_index, offset, half, row_scale),
        out_shape=(
            jax.ShapeDtypeStruct((4 * rows, latents), jnp.float32),
            jax.ShapeDtypeStruct((out_rows, wide), jnp.float32),
            jax.ShapeDtypeStruct((latents, 2 * half), jnp.bfloat16),
        ),
        in_specs=[SMEM] + [VMEM] * 7 + ([VMEM, HBM] if later else []),
        out_specs=(VMEM, VMEM, HBM),
        scratch_shapes=[
            pltpu.VMEM((latents, wide), jnp.bfloat16),
            pltpu.SemaphoreType.DMA((len(chunks(wide)),)),
        ],
        input_output_aliases={9: 2} if later else {},
        compiler_params=params(SMALL_VMEM),
        cost_estimate=estimate(16 * rows * latents * wide, 4 * latents * wide),
        name="grad",
    )(core, left, scale, dec, *blocks, *(held if later else ()))


def tail_kernel(widths, row_scale, groups, core_ref, left_ref, scale_ref, norm_ref, total_ref, dec_ref, *refs):
    count = len(widths)
    preacts, refs = refs[:groups], refs[groups:]
    recons, refs = refs[: 2 * count - 1], refs[2 * count - 1 :]
    e_blocks, refs = refs[:4], refs[4:]
    x_blocks, refs = [refs[4 * k : 4 * k + 4] for k in range(2 * count)], refs[8 * count + 1 :]
    dec_grad_ref, enc_grad_ref, bias_ref, recon_ref = refs[:4]
    dec_out, enc_out, recon_last, pre_ref, dec_sems, enc_sems = refs[4:]
    core = core_ref[0]
    half = sum(widths)
    bases = []
    for k in range(2 * count):
        side_index, q = divmod(k, count)
        bases.append(piece_base(core, half, side_index, sum(widths[:q])))
    err = stack(e_blocks)
    outs = []

    def product():
        return lax.dot_general(err, dec_ref[...], (((1,), (1,)), ((), ())), preferred_element_type=jnp.float32)

    def use(result):
        act_grad = total_ref[...] + result + norm_ref[...]
        rounded = jnp.where(stack(preacts) > 0.0, act_grad, 0.0).astype(jnp.bfloat16)
        pre_ref[...] = rounded
        bias_ref[...] = jnp.sum(rounded.astype(jnp.float32), axis=0, keepdims=True)

    def encoder_task(spot, row, k, at, step):
        def product():
            mine = jnp.concatenate([ref[:, at : at + step] for ref in x_blocks[k]], axis=0)
            return lax.dot_general(mine, pre_ref[...], (((0,), (0,)), ((), ())), preferred_element_type=jnp.float32)

        def use(piece):
            enc_out[row : row + step] = piece.astype(jnp.bfloat16)
            start = pl.multiple_of(bases[k] + at, 128)
            out = pltpu.make_async_copy(
                enc_out.at[pl.ds(row, step), :], enc_grad_ref.at[pl.ds(start, step), :], enc_sems.at[spot]
            )
            out.start()
            outs.append(out)

        return product, use

    decoder = decoder_tasks(
        bases[-1], row_scale, left_ref, scale_ref, dec_ref, err, dec_out, dec_grad_ref, recon_last, dec_sems, outs
    )
    encoder = []
    row = 0
    for k in range(2 * count):
        for at, step in chunks(widths[k % count]):
            encoder.append(encoder_task(len(encoder), row, k, at, step))
            row += step
    tasks = [(product, use), decoder.pop(0)]
    for spot, task in enumerate(encoder):
        tasks.append(task)
        if decoder and spot % 2 == 1:
            tasks.append(decoder.pop(0))
    pipelined(tasks)
    for k, held in enumerate(list(recons) + [recon_last]):
        recon_ref[:, pl.ds(pl.multiple_of(bases[k], 128), widths[k % count])] = held[...]
    for out in outs:
        out.wait()


def tail(core, left, preacts, scale, norm, total, dec, recons, e_blocks, x_blocks, dec_grad, row_scale, widths):
    rows = e_blocks[0].shape[0]
    latents = dec.shape[0]
    half = sum(widths)
    out_rows = recons[0].shape[0]
    spots = 2 * sum(len(chunks(w)) for w in widths)
    vmem_args = [left, scale, norm, total, dec, *preacts, *recons, *e_blocks, *[b for blocks in x_blocks for b in blocks]]
    return pl.pallas_call(
        functools.partial(tail_kernel, widths, row_scale, len(preacts)),
        out_shape=(
            jax.ShapeDtypeStruct((latents, 2 * half), jnp.bfloat16),
            jax.ShapeDtypeStruct((2 * half, latents), jnp.bfloat16),
            jax.ShapeDtypeStruct((1, latents), jnp.float32),
            jax.ShapeDtypeStruct((out_rows, 2 * half), jnp.float32),
        ),
        in_specs=[SMEM] + [VMEM] * len(vmem_args) + [HBM],
        out_specs=(HBM, HBM, VMEM, VMEM),
        scratch_shapes=[
            pltpu.VMEM((latents, widths[-1]), jnp.bfloat16),
            pltpu.VMEM((2 * half, latents), jnp.bfloat16),
            pltpu.VMEM((out_rows, widths[-1]), jnp.float32),
            pltpu.VMEM((4 * rows, latents), jnp.bfloat16),
            pltpu.SemaphoreType.DMA((len(chunks(widths[-1])),)),
            pltpu.SemaphoreType.DMA((spots,)),
        ],
        input_output_aliases={1 + len(vmem_args): 0},
        compiler_params=params(TAIL_VMEM),
        cost_estimate=estimate(24 * rows * latents * half, 8 * latents * half),
        name="tail",
    )(core, *vmem_args, dec_grad)


def per_device(tokens, batch_order, enc_weight, enc_bias, dec_weight):
    rows_dev, width = tokens.shape
    total_rows = batch_order.shape[0]
    row_scale = math.sqrt(total_rows)
    half = width // 2
    widths = (half,)
    block_rows = total_rows // 4
    core = lax.axis_index("c")
    core_arg = core[None].astype(jnp.int32)

    got = swap_cores(tokens)
    low = jnp.concatenate([tokens[:, :half], got[:, :half]])
    high = jnp.concatenate([got[:, half:], tokens[:, half:]])
    block = jnp.where(core == 0, low, high)
    near = near_copies(block)
    x_own = spread(near)
    encs, decs = load(core_arg, near, enc_weight, dec_weight, widths)
    done = []

    def work(group):
        oth = [swap_cores(x_own[k]) for k in group]
        pre_part, act, sibling = front([x_own[k] for k in group], oth, encs, enc_bias, decs[1])
        own = parts(act, decs[0], len(group))
        done.append((oth, pre_part, act, sibling, own))

    work(GROUPS[0])
    x_own[1:], encs, decs, done[0] = lax.optimization_barrier((x_own[1:], encs, decs, done[0]))
    for group in GROUPS[1:]:
        work(group)
    preacts, acts = [item[1] for item in done], [item[2] for item in done]
    x_oth, parts_oth, parts_own = [[a for item in done for a in item[k]] for k in (0, 3, 4)]
    got = [swap_cores(part) for part in parts_oth]
    total = parts_own[0].astype(jnp.float32) + got[0].astype(jnp.float32)
    for k in range(1, 4):
        sent = (parts_own[k].astype(jnp.float32) + got[k].astype(jnp.float32)).astype(jnp.bfloat16)
        total = total + lax.ppermute(sent, NAMES, SHIFTS[k - 1]).astype(jnp.float32)
    left, scale, norm = side(batch_order, acts, decs, row_scale, rows_dev)
    total = total.astype(jnp.bfloat16).reshape(16, block_rows // 16, half)
    total, left, scale, norm = lax.optimization_barrier((total, left, scale, norm))
    pieces = lax.all_to_all(total, CHIPS, 0, 0, axis_index_groups=CLASSES)
    recon = jnp.sum(pieces.astype(jnp.float32), axis=0) - block.astype(jnp.float32)
    err_block = (recon / row_scale).astype(jnp.bfloat16)
    near = near_copies(err_block)
    e_own = spread(near)
    e_oth = [swap_cores(a) for a in e_own]
    act_part, recon_own, dec_grad = grad(core_arg, left, scale, decs[0], e_own, None, 0, 0, half, row_scale, rows_dev)
    dec_grad, enc_grad, bias_grad, recon_error = tail(
        core_arg, left, preacts, scale, norm, act_part, decs[1], [recon_own], e_oth, [x_own, x_oth], dec_grad, row_scale,
        widths,
    )
    return (recon_error, enc_grad, dec_grad, bias_grad[0])


def solution(mesh):
    split = Mesh(mesh.devices.reshape(4, 2, 2, 4, 2), NAMES)
    return jax.shard_map(
        per_device,
        mesh=split,
        in_specs=(P(NAMES, None), P(), P(None, NAMES), P(NAMES), P(NAMES, None)),
        out_specs=(P(NAMES, None), P(None, NAMES), P(NAMES, None), P(NAMES)),
        check_vma=False,
    )
```

```python
import functools
import itertools
import math

import jax
import jax.numpy as jnp
from jax import lax
from jax.experimental import pallas as pl
from jax.experimental.pallas import tpu as pltpu
from jax.sharding import Mesh, PartitionSpec as P

CHIPS = ("z", "xh", "xl", "y")
NAMES = CHIPS + ("c",)
SWAP = [(0, 1), (1, 0)]
SMALL_VMEM = 12 * 2**20
TAIL_VMEM = 20 * 2**20
SMEM = pl.BlockSpec(memory_space=pltpu.SMEM)
VMEM = pl.BlockSpec(memory_space=pltpu.VMEM)
ANY = pl.BlockSpec(memory_space=pl.ANY)
HBM = pl.BlockSpec(memory_space=pltpu.HBM)


def chip_index(z, x, y):
    return ((z % 4) * 4 + x % 4) * 4 + y % 4


def chip_classes():
    groups = []
    for b, a in itertools.product(range(2), range(2)):
        group = []
        for z, x, y in itertools.product(range(4), range(2), range(2)):
            group.append(chip_index(z, 2 * x + (a + z) % 2, 2 * y + (b + z) % 2))
        groups.append(group)
    return groups


def neighbour_shifts():
    shifts = []
    for step in ((0, 1, 0), (0, 0, 1), (1, 0, 0)):
        pairs = []
        for z, x, y in itertools.product(range(4), repeat=3):
            for c in range(2):
                s = 1 - 2 * c
                to = chip_index(z + s * step[0], x + s * step[1], y + s * step[2])
                pairs.append((chip_index(z, x, y) * 2 + c, to * 2 + c))
        shifts.append(pairs)
    return shifts


CLASSES = chip_classes()
SHIFTS = neighbour_shifts()
GROUPS = ((0,), (1,), (2, 3))


def near_copies(block):
    copies = jnp.broadcast_to(block[None], (16,) + block.shape)
    near = lax.all_to_all(copies, CHIPS, 0, 0, axis_index_groups=CLASSES)
    return near.reshape(16 * block.shape[0], block.shape[1])


def spread(near):
    return [near] + [lax.ppermute(near, NAMES, pairs) for pairs in SHIFTS]


def swap_cores(a):
    return lax.ppermute(a, "c", SWAP)


def stack(blocks):
    return jnp.concatenate([ref[...] for ref in blocks], axis=0)


def estimate(flops, moved):
    return pl.CostEstimate(flops=flops, bytes_accessed=moved, transcendentals=0)


def params(limit):
    return pltpu.CompilerParams(vmem_limit_bytes=limit)


def chunks(width):
    found, at = [], 0
    while at < width:
        step = min(768, width - at)
        if width - at == 1024:
            step = 512
        found.append((at, step))
        at += step
    return found


def load_kernel(widths, core_ref, near_ref, enc_ref, dec_ref, *refs):
    pieces = 2 * len(widths)
    enc_refs, dec_refs, sems = refs[:pieces], refs[pieces : 2 * pieces], refs[2 * pieces]
    half = sum(widths)
    copies = []
    for k in range(pieces):
        side_index, q = divmod(k, len(widths))
        base = jnp.where(core_ref[0] == side_index, 0, half) + sum(widths[:q])
        base = pl.multiple_of(base, 128)
        cut = pl.ds(base, widths[q])
        copies.append(pltpu.make_async_copy(enc_ref.at[cut, :], enc_refs[k], sems.at[k, 0]))
        copies.append(pltpu.make_async_copy(dec_ref.at[:, cut], dec_refs[k], sems.at[k, 1]))
    for copy in copies:
        copy.start()
    for copy in copies:
        copy.wait()


def load(core, near, enc_weight, dec_weight, widths):
    width, latents = enc_weight.shape
    both = list(widths) * 2
    out = pl.pallas_call(
        functools.partial(load_kernel, widths),
        out_shape=[jax.ShapeDtypeStruct((w, latents), jnp.bfloat16) for w in both]
        + [jax.ShapeDtypeStruct((latents, w), jnp.bfloat16) for w in both],
        in_specs=[SMEM, ANY, HBM, HBM],
        out_specs=[VMEM] * (2 * len(both)),
        scratch_shapes=[pltpu.SemaphoreType.DMA((len(both), 2))],
        compiler_params=params(SMALL_VMEM),
        cost_estimate=estimate(0, 8 * width * latents),
        name="load",
    )(core, near, enc_weight, dec_weight)
    return out[: len(both)], out[len(both) :]


def pipelined(tasks):
    held = None
    for product, use in tasks:
        result = product()
        if held is not None:
            held[0](held[1])
        held = (use, result)
    held[0](held[1])


def part_tasks(act_ref, dec_ref, part_refs):
    rows = part_refs[0].shape[0]

    def task(cols):
        def product():
            return jnp.dot(act_ref[...], dec_ref[:, cols], preferred_element_type=jnp.float32)

        def use(result):
            result = result.astype(jnp.bfloat16)
            for b, ref in enumerate(part_refs):
                ref[:, cols] = result[b * rows : (b + 1) * rows]

        return product, use

    return [task(slice(at, at + step)) for at, step in chunks(dec_ref.shape[1])]


def front_kernel(count, bias_ref, enc_own, enc_oth, dec_ref, *refs):
    x_own, x_oth = refs[:count], refs[count : 2 * count]
    preact_ref, act_ref = refs[2 * count : 2 * count + 2]
    preact = jnp.dot(stack(x_own), enc_own[...], preferred_element_type=jnp.float32)
    preact = preact + jnp.dot(stack(x_oth), enc_oth[...], preferred_element_type=jnp.float32) + bias_ref[...]
    preact_ref[...] = preact
    act_ref[...] = jnp.maximum(preact, 0.0).astype(jnp.bfloat16)
    pipelined(part_tasks(act_ref, dec_ref, refs[2 * count + 2 :]))


def front(x_own, x_oth, encs, enc_bias, dec):
    count = len(x_own)
    rows, half = x_own[0].shape
    latents = dec.shape[0]
    out = pl.pallas_call(
        functools.partial(front_kernel, count),
        out_shape=[
            jax.ShapeDtypeStruct((count * rows, latents), jnp.float32),
            jax.ShapeDtypeStruct((count * rows, latents), jnp.bfloat16),
        ]
        + [jax.ShapeDtypeStruct((rows, half), jnp.bfloat16)] * count,
        in_specs=[VMEM] * (4 + 2 * count),
        out_specs=[VMEM] * (2 + count),
        compiler_params=params(SMALL_VMEM),
        cost_estimate=estimate(6 * count * rows * latents * half, 8 * latents * half),
        name="front",
    )(enc_bias[None], *encs, dec, *x_own, *x_oth)
    return out[0], out[1], out[2:]


def parts_kernel(act_ref, dec_ref, *part_refs):
    pipelined(part_tasks(act_ref, dec_ref, part_refs))


def parts(act, dec, count):
    total_rows, latents = act.shape
    wide = dec.shape[1]
    return pl.pallas_call(
        parts_kernel,
        out_shape=[jax.ShapeDtypeStruct((total_rows // count, wide), jnp.bfloat16)] * count,
        in_specs=[VMEM] * 2,
        out_specs=[VMEM] * count,
        compiler_params=params(SMALL_VMEM),
        cost_estimate=estimate(2 * total_rows * latents * wide, 4 * latents * wide),
        name="parts",
    )(act, dec)


def side_kernel(row_scale, rows_dev, groups, order_ref, *refs):
    acts, decs, (left_ref, scale_ref, norm_ref) = refs[:groups], refs[groups:-3], refs[-3:]
    act = stack(acts)
    total_rows, latents = act.shape
    left_ref[:latents] = act.T
    spot = lax.broadcasted_iota(jnp.int32, (16, total_rows), 0)
    target = jnp.full((16, total_rows), -1, jnp.int32)
    z = lax.axis_index("z")
    x = lax.axis_index("xh") * 2 + lax.axis_index("xl")
    y = lax.axis_index("y")
    first = (((z * 4 + x) * 4 + y) * 2 + lax.axis_index("c")) * rows_dev
    chip_rows = 2 * rows_dev
    for r in range(rows_dev):
        wanted = order_ref[first + r]
        chip = wanted // chip_rows
        tz, tx, ty = chip // 16, chip // 4 % 4, chip % 4
        kind = (tx + tz + x + z) % 2 + 2 * ((ty + tz + y + z) % 2)
        place = (kind * 16 + tz * 4 + tx // 2 * 2 + ty // 2) * chip_rows + wanted % chip_rows
        target = jnp.where(spot == r, place, target)
    chosen = lax.broadcasted_iota(jnp.int32, (16, total_rows), 1) == target
    left_ref[latents:] = jnp.where(chosen, 1.0, 0.0).astype(jnp.bfloat16)
    total = jnp.sum(act.astype(jnp.float32), axis=0, keepdims=True) / row_scale
    total = jnp.broadcast_to(total, (128, latents)).T[:, :1]
    squares = jnp.zeros((latents, 128), jnp.float32)
    for dec in decs:
        for c in range(dec.shape[1] // 128):
            wide = dec[:, c * 128 : (c + 1) * 128].astype(jnp.float32)
            squares = squares + wide * wide
    norms = jnp.sqrt(jnp.sum(squares, axis=1, keepdims=True) + 1e-06)
    scale_ref[...] = total / norms
    norm_ref[...] = jnp.broadcast_to(norms / row_scale, (latents, 128)).T[:1]


def side(order, acts, decs, row_scale, rows_dev):
    total_rows, latents = sum(act.shape[0] for act in acts), acts[0].shape[1]
    width = sum(dec.shape[1] for dec in decs)
    return pl.pallas_call(
        functools.partial(side_kernel, row_scale, rows_dev, len(acts)),
        out_shape=(
            jax.ShapeDtypeStruct((latents + 16, total_rows), jnp.bfloat16),
            jax.ShapeDtypeStruct((latents, 1), jnp.float32),
            jax.ShapeDtypeStruct((1, latents), jnp.float32),
        ),
        in_specs=[SMEM] + [VMEM] * (len(acts) + len(decs)),
        out_specs=(VMEM, VMEM, VMEM),
        compiler_params=params(SMALL_VMEM),
        cost_estimate=estimate(4 * latents * width, 2 * latents * width),
        name="side",
    )(order, *acts, *decs)


def decoder_tasks(base, row_scale, left_ref, scale_ref, dec_ref, err, dec_out, dec_grad_ref, recon_ref, sems, outs):
    latents, wide = dec_ref.shape

    def task(spot, at, step):
        cols = slice(at, at + step)

        def product():
            return jnp.dot(left_ref[...], err[:, cols], preferred_element_type=jnp.float32)

        def use(both):
            grad = both[:latents] + scale_ref[...] * dec_ref[:, cols].astype(jnp.float32)
            dec_out[:, cols] = grad.astype(jnp.bfloat16)
            recon_ref[:, cols] = both[latents : latents + recon_ref.shape[0]] * row_scale
            start = pl.multiple_of(base + at, 128)
            out = pltpu.make_async_copy(dec_out.at[:, cols], dec_grad_ref.at[:, pl.ds(start, step)], sems.at[spot])
            out.start()
            outs.append(out)

        return product, use

    return [task(spot, at, step) for spot, (at, step) in enumerate(chunks(wide))]


def piece_base(core, half, side_index, offset):
    return jnp.where(core == side_index, 0, half) + offset


def grad_kernel(later, side_index, offset, half, row_scale, core_ref, left_ref, scale_ref, dec_ref, *refs):
    blocks, refs = refs[:4], refs[4:]
    before, refs = (refs[0], refs[2:]) if later else (None, refs)
    total_ref, recon_ref, dec_grad_ref, dec_out, sems = refs
    base = piece_base(core_ref[0], half, side_index, offset)
    err = stack(blocks)
    outs = []

    def product():
        return lax.dot_general(err, dec_ref[...], (((1,), (1,)), ((), ())), preferred_element_type=jnp.float32)

    def use(result):
        total_ref[...] = before[...] + result if later else result

    pipelined(
        decoder_tasks(base, row_scale, left_ref, scale_ref, dec_ref, err, dec_out, dec_grad_ref, recon_ref, sems, outs)
        + [(product, use)]
    )
    for out in outs:
        out.wait()


def grad(core, left, scale, dec, blocks, held, side_index, offset, half, row_scale, out_rows):
    rows, wide = blocks[0].shape
    latents = dec.shape[0]
    later = held is not None
    return pl.pallas_call(
        functools.partial(grad_kernel, later, side_index, offset, half, row_scale),
        out_shape=(
            jax.ShapeDtypeStruct((4 * rows, latents), jnp.float32),
            jax.ShapeDtypeStruct((out_rows, wide), jnp.float32),
            jax.ShapeDtypeStruct((latents, 2 * half), jnp.bfloat16),
        ),
        in_specs=[SMEM] + [VMEM] * 7 + ([VMEM, HBM] if later else []),
        out_specs=(VMEM, VMEM, HBM),
        scratch_shapes=[
            pltpu.VMEM((latents, wide), jnp.bfloat16),
            pltpu.SemaphoreType.DMA((len(chunks(wide)),)),
        ],
        input_output_aliases={9: 2} if later else {},
        compiler_params=params(SMALL_VMEM),
        cost_estimate=estimate(16 * rows * latents * wide, 4 * latents * wide),
        name="grad",
    )(core, left, scale, dec, *blocks, *(held if later else ()))


def tail_kernel(widths, row_scale, groups, core_ref, left_ref, scale_ref, norm_ref, total_ref, dec_ref, *refs):
    count = len(widths)
    preacts, refs = refs[:groups], refs[groups:]
    recons, refs = refs[: 2 * count - 1], refs[2 * count - 1 :]
    e_blocks, refs = refs[:4], refs[4:]
    x_blocks, refs = [refs[4 * k : 4 * k + 4] for k in range(2 * count)], refs[8 * count + 1 :]
    dec_grad_ref, enc_grad_ref, bias_ref, recon_ref = refs[:4]
    dec_out, enc_out, recon_last, pre_ref, dec_sems, enc_sems = refs[4:]
    core = core_ref[0]
    half = sum(widths)
    bases = []
    for k in range(2 * count):
        side_index, q = divmod(k, count)
        bases.append(piece_base(core, half, side_index, sum(widths[:q])))
    err = stack(e_blocks)
    outs = []

    def product():
        return lax.dot_general(err, dec_ref[...], (((1,), (1,)), ((), ())), preferred_element_type=jnp.float32)

    def use(result):
        act_grad = total_ref[...] + result + norm_ref[...]
        rounded = jnp.where(stack(preacts) > 0.0, act_grad, 0.0).astype(jnp.bfloat16)
        pre_ref[...] = rounded
        bias_ref[...] = jnp.sum(rounded.astype(jnp.float32), axis=0, keepdims=True)

    def encoder_task(spot, row, k, at, step):
        def product():
            mine = jnp.concatenate([ref[:, at : at + step] for ref in x_blocks[k]], axis=0)
            return lax.dot_general(mine, pre_ref[...], (((0,), (0,)), ((), ())), preferred_element_type=jnp.float32)

        def use(piece):
            enc_out[row : row + step] = piece.astype(jnp.bfloat16)
            start = pl.multiple_of(bases[k] + at, 128)
            out = pltpu.make_async_copy(
                enc_out.at[pl.ds(row, step), :], enc_grad_ref.at[pl.ds(start, step), :], enc_sems.at[spot]
            )
            out.start()
            outs.append(out)

        return product, use

    decoder = decoder_tasks(
        bases[-1], row_scale, left_ref, scale_ref, dec_ref, err, dec_out, dec_grad_ref, recon_last, dec_sems, outs
    )
    encoder = []
    row = 0
    for k in range(2 * count):
        for at, step in chunks(widths[k % count]):
            encoder.append(encoder_task(len(encoder), row, k, at, step))
            row += step
    tasks = [(product, use), decoder.pop(0)]
    for spot, task in enumerate(encoder):
        tasks.append(task)
        if decoder and spot % 2 == 1:
            tasks.append(decoder.pop(0))
    pipelined(tasks)
    for k, held in enumerate(list(recons) + [recon_last]):
        recon_ref[:, pl.ds(pl.multiple_of(bases[k], 128), widths[k % count])] = held[...]
    for out in outs:
        out.wait()


def tail(core, left, preacts, scale, norm, total, dec, recons, e_blocks, x_blocks, dec_grad, row_scale, widths):
    rows = e_blocks[0].shape[0]
    latents = dec.shape[0]
    half = sum(widths)
    out_rows = recons[0].shape[0]
    spots = 2 * sum(len(chunks(w)) for w in widths)
    vmem_args = [left, scale, norm, total, dec, *preacts, *recons, *e_blocks, *[b for blocks in x_blocks for b in blocks]]
    return pl.pallas_call(
        functools.partial(tail_kernel, widths, row_scale, len(preacts)),
        out_shape=(
            jax.ShapeDtypeStruct((latents, 2 * half), jnp.bfloat16),
            jax.ShapeDtypeStruct((2 * half, latents), jnp.bfloat16),
            jax.ShapeDtypeStruct((1, latents), jnp.float32),
            jax.ShapeDtypeStruct((out_rows, 2 * half), jnp.float32),
        ),
        in_specs=[SMEM] + [VMEM] * len(vmem_args) + [HBM],
        out_specs=(HBM, HBM, VMEM, VMEM),
        scratch_shapes=[
            pltpu.VMEM((latents, widths[-1]), jnp.bfloat16),
            pltpu.VMEM((2 * half, latents), jnp.bfloat16),
            pltpu.VMEM((out_rows, widths[-1]), jnp.float32),
            pltpu.VMEM((4 * rows, latents), jnp.bfloat16),
            pltpu.SemaphoreType.DMA((len(chunks(widths[-1])),)),
            pltpu.SemaphoreType.DMA((spots,)),
        ],
        input_output_aliases={1 + len(vmem_args): 0},
        compiler_params=params(TAIL_VMEM),
        cost_estimate=estimate(24 * rows * latents * half, 8 * latents * half),
        name="tail",
    )(core, *vmem_args, dec_grad)


def per_device(tokens, batch_order, enc_weight, enc_bias, dec_weight):
    rows_dev, width = tokens.shape
    total_rows = batch_order.shape[0]
    row_scale = math.sqrt(total_rows)
    half = width // 2
    widths = (half,)
    block_rows = total_rows // 4
    core = lax.axis_index("c")
    core_arg = core[None].astype(jnp.int32)

    got = swap_cores(tokens)
    low = jnp.concatenate([tokens[:, :half], got[:, :half]])
    high = jnp.concatenate([got[:, half:], tokens[:, half:]])
    block = jnp.where(core == 0, low, high)
    near = near_copies(block)
    x_own = spread(near)
    encs, decs = load(core_arg, near, enc_weight, dec_weight, widths)
    done = []

    def work(group):
        oth = [swap_cores(x_own[k]) for k in group]
        pre_part, act, sibling = front([x_own[k] for k in group], oth, encs, enc_bias, decs[1])
        own = parts(act, decs[0], len(group))
        done.append((oth, pre_part, act, sibling, own))

    work(GROUPS[0])
    x_own[1:], encs, decs, done[0] = lax.optimization_barrier((x_own[1:], encs, decs, done[0]))
    for group in GROUPS[1:]:
        work(group)
    preacts, acts = [item[1] for item in done], [item[2] for item in done]
    x_oth, parts_oth, parts_own = [[a for item in done for a in item[k]] for k in (0, 3, 4)]
    got = [swap_cores(part) for part in parts_oth]
    total = parts_own[0].astype(jnp.float32) + got[0].astype(jnp.float32)
    for k in range(1, 4):
        sent = (parts_own[k].astype(jnp.float32) + got[k].astype(jnp.float32)).astype(jnp.bfloat16)
        total = total + lax.ppermute(sent, NAMES, SHIFTS[k - 1]).astype(jnp.float32)
    left, scale, norm = side(batch_order, acts, decs, row_scale, rows_dev)
    total = total.astype(jnp.bfloat16).reshape(16, block_rows // 16, half)
    total, left, scale, norm = lax.optimization_barrier((total, left, scale, norm))
    pieces = lax.all_to_all(total, CHIPS, 0, 0, axis_index_groups=CLASSES)
    recon = jnp.sum(pieces.astype(jnp.float32), axis=0) - block.astype(jnp.float32)
    err_block = (recon / row_scale).astype(jnp.bfloat16)
    near = near_copies(err_block)
    e_own = spread(near)
    e_oth = [swap_cores(a) for a in e_own]
    act_part, recon_own, dec_grad = grad(core_arg, left, scale, decs[0], e_own, None, 0, 0, half, row_scale, rows_dev)
    dec_grad, enc_grad, bias_grad, recon_error = tail(
        core_arg, left, preacts, scale, norm, act_part, decs[1], [recon_own], e_oth, [x_own, x_oth], dec_grad, row_scale,
        widths,
    )
    return (recon_error, enc_grad, dec_grad, bias_grad[0])


def solution(mesh):
    split = Mesh(mesh.devices.reshape(4, 2, 2, 4, 2), NAMES)
    return jax.shard_map(
        per_device,
        mesh=split,
        in_specs=(P(NAMES, None), P(), P(None, NAMES), P(NAMES), P(NAMES, None)),
        out_specs=(P(NAMES, None), P(None, NAMES), P(NAMES, None), P(NAMES)),
        check_vma=False,
    )
```

```python
import functools
import itertools
import math

import jax
import jax.numpy as jnp
from jax import lax
from jax.experimental import pallas as pl
from jax.experimental.pallas import tpu as pltpu
from jax.sharding import Mesh, PartitionSpec as P

CHIPS = ("z", "xh", "xl", "y")
NAMES = CHIPS + ("c",)
SWAP = [(0, 1), (1, 0)]
SMALL_VMEM = 12 * 2**20
TAIL_VMEM = 20 * 2**20
SMEM = pl.BlockSpec(memory_space=pltpu.SMEM)
VMEM = pl.BlockSpec(memory_space=pltpu.VMEM)
ANY = pl.BlockSpec(memory_space=pl.ANY)
HBM = pl.BlockSpec(memory_space=pltpu.HBM)


def chip_index(z, x, y):
    return ((z % 4) * 4 + x % 4) * 4 + y % 4


def chip_classes():
    groups = []
    for b, a in itertools.product(range(2), range(2)):
        group = []
        for z, x, y in itertools.product(range(4), range(2), range(2)):
            group.append(chip_index(z, 2 * x + (a + z) % 2, 2 * y + (b + z) % 2))
        groups.append(group)
    return groups


def neighbour_shifts():
    shifts = []
    for step in ((0, 1, 0), (0, 0, 1), (1, 0, 0)):
        pairs = []
        for z, x, y in itertools.product(range(4), repeat=3):
            for c in range(2):
                s = 1 - 2 * c
                to = chip_index(z + s * step[0], x + s * step[1], y + s * step[2])
                pairs.append((chip_index(z, x, y) * 2 + c, to * 2 + c))
        shifts.append(pairs)
    return shifts


CLASSES = chip_classes()
SHIFTS = neighbour_shifts()
GROUPS = ((0,), (1,), (2, 3))


def near_copies(block):
    copies = jnp.broadcast_to(block[None], (16,) + block.shape)
    near = lax.all_to_all(copies, CHIPS, 0, 0, axis_index_groups=CLASSES)
    return near.reshape(16 * block.shape[0], block.shape[1])


def spread(near):
    return [near] + [lax.ppermute(near, NAMES, pairs) for pairs in SHIFTS]


def swap_cores(a):
    return lax.ppermute(a, "c", SWAP)


def stack(blocks):
    return jnp.concatenate([ref[...] for ref in blocks], axis=0)


def estimate(flops, moved):
    return pl.CostEstimate(flops=flops, bytes_accessed=moved, transcendentals=0)


def params(limit):
    return pltpu.CompilerParams(vmem_limit_bytes=limit)


def chunks(width):
    found, at = [], 0
    while at < width:
        step = min(768, width - at)
        if width - at == 1024:
            step = 512
        found.append((at, step))
        at += step
    return found


def load_kernel(widths, near_ref, enc_ref, dec_ref, *refs):
    pieces = 2 * len(widths)
    enc_refs, dec_refs, sems = refs[:pieces], refs[pieces : 2 * pieces], refs[2 * pieces]
    half = sum(widths)
    copies = []
    for k in range(pieces):
        side_index, q = divmod(k, len(widths))
        base = piece_base(lax.axis_index("c"), half, side_index, sum(widths[:q]))
        base = pl.multiple_of(base, 128)
        cut = pl.ds(base, widths[q])
        copies.append(pltpu.make_async_copy(enc_ref.at[cut, :], enc_refs[k], sems.at[k, 0]))
        copies.append(pltpu.make_async_copy(dec_ref.at[:, cut], dec_refs[k], sems.at[k, 1]))
    for copy in copies:
        copy.start()
    for copy in copies:
        copy.wait()


def load(near, enc_weight, dec_weight, widths):
    width, latents = enc_weight.shape
    both = list(widths) * 2
    out = pl.pallas_call(
        functools.partial(load_kernel, widths),
        out_shape=[jax.ShapeDtypeStruct((w, latents), jnp.bfloat16) for w in both]
        + [jax.ShapeDtypeStruct((latents, w), jnp.bfloat16) for w in both],
        in_specs=[ANY, HBM, HBM],
        out_specs=[VMEM] * (2 * len(both)),
        scratch_shapes=[pltpu.SemaphoreType.DMA((len(both), 2))],
        compiler_params=params(SMALL_VMEM),
        cost_estimate=estimate(0, 8 * width * latents),
        name="load",
    )(near, enc_weight, dec_weight)
    return out[: len(both)], out[len(both) :]


def pipelined(tasks):
    held = None
    for product, use in tasks:
        result = product()
        if held is not None:
            held[0](held[1])
        held = (use, result)
    held[0](held[1])


def part_tasks(act_ref, dec_ref, part_refs):
    rows = part_refs[0].shape[0]

    def task(cols):
        def product():
            return jnp.dot(act_ref[...], dec_ref[:, cols], preferred_element_type=jnp.float32)

        def use(result):
            result = result.astype(jnp.bfloat16)
            for b, ref in enumerate(part_refs):
                ref[:, cols] = result[b * rows : (b + 1) * rows]

        return product, use

    return [task(slice(at, at + step)) for at, step in chunks(dec_ref.shape[1])]


def front_kernel(count, bias_ref, enc_own, enc_oth, dec_ref, *refs):
    x_own, x_oth = refs[:count], refs[count : 2 * count]
    preact_ref, act_ref = refs[2 * count : 2 * count + 2]
    preact = jnp.dot(stack(x_own), enc_own[...], preferred_element_type=jnp.float32)
    preact = preact + jnp.dot(stack(x_oth), enc_oth[...], preferred_element_type=jnp.float32) + bias_ref[...]
    preact_ref[...] = preact
    act_ref[...] = jnp.maximum(preact, 0.0).astype(jnp.bfloat16)
    pipelined(part_tasks(act_ref, dec_ref, refs[2 * count + 2 :]))


def front(x_own, x_oth, encs, enc_bias, dec):
    count = len(x_own)
    rows, half = x_own[0].shape
    latents = dec.shape[0]
    out = pl.pallas_call(
        functools.partial(front_kernel, count),
        out_shape=[
            jax.ShapeDtypeStruct((count * rows, latents), jnp.float32),
            jax.ShapeDtypeStruct((count * rows, latents), jnp.bfloat16),
        ]
        + [jax.ShapeDtypeStruct((rows, half), jnp.bfloat16)] * count,
        in_specs=[VMEM] * (4 + 2 * count),
        out_specs=[VMEM] * (2 + count),
        compiler_params=params(SMALL_VMEM),
        cost_estimate=estimate(6 * count * rows * latents * half, 8 * latents * half),
        name="front",
    )(enc_bias[None], *encs, dec, *x_own, *x_oth)
    return out[0], out[1], out[2:]


def parts_kernel(act_ref, dec_ref, *part_refs):
    pipelined(part_tasks(act_ref, dec_ref, part_refs))


def parts(act, dec, count):
    total_rows, latents = act.shape
    wide = dec.shape[1]
    return pl.pallas_call(
        parts_kernel,
        out_shape=[jax.ShapeDtypeStruct((total_rows // count, wide), jnp.bfloat16)] * count,
        in_specs=[VMEM] * 2,
        out_specs=[VMEM] * count,
        compiler_params=params(SMALL_VMEM),
        cost_estimate=estimate(2 * total_rows * latents * wide, 4 * latents * wide),
        name="parts",
    )(act, dec)


def side_kernel(row_scale, rows_dev, groups, order_ref, *refs):
    acts, decs, (left_ref, scale_ref, norm_ref) = refs[:groups], refs[groups:-3], refs[-3:]
    act = stack(acts)
    total_rows, latents = act.shape
    left_ref[:latents] = act.T
    spot = lax.broadcasted_iota(jnp.int32, (16, total_rows), 0)
    target = jnp.full((16, total_rows), -1, jnp.int32)
    z = lax.axis_index("z")
    x = lax.axis_index("xh") * 2 + lax.axis_index("xl")
    y = lax.axis_index("y")
    first = (((z * 4 + x) * 4 + y) * 2 + lax.axis_index("c")) * rows_dev
    chip_rows = 2 * rows_dev
    for r in range(rows_dev):
        wanted = order_ref[first + r]
        chip = wanted // chip_rows
        tz, tx, ty = chip // 16, chip // 4 % 4, chip % 4
        kind = (tx + tz + x + z) % 2 + 2 * ((ty + tz + y + z) % 2)
        place = (kind * 16 + tz * 4 + tx // 2 * 2 + ty // 2) * chip_rows + wanted % chip_rows
        target = jnp.where(spot == r, place, target)
    chosen = lax.broadcasted_iota(jnp.int32, (16, total_rows), 1) == target
    left_ref[latents:] = jnp.where(chosen, 1.0, 0.0).astype(jnp.bfloat16)
    total = jnp.sum(act.astype(jnp.float32), axis=0, keepdims=True) / row_scale
    total = jnp.broadcast_to(total, (128, latents)).T[:, :1]
    squares = jnp.zeros((latents, 128), jnp.float32)
    for dec in decs:
        for c in range(dec.shape[1] // 128):
            wide = dec[:, c * 128 : (c + 1) * 128].astype(jnp.float32)
            squares = squares + wide * wide
    norms = jnp.sqrt(jnp.sum(squares, axis=1, keepdims=True) + 1e-06)
    scale_ref[...] = total / norms
    norm_ref[...] = jnp.broadcast_to(norms / row_scale, (latents, 128)).T[:1]


def side(order, acts, decs, row_scale, rows_dev):
    total_rows, latents = sum(act.shape[0] for act in acts), acts[0].shape[1]
    width = sum(dec.shape[1] for dec in decs)
    return pl.pallas_call(
        functools.partial(side_kernel, row_scale, rows_dev, len(acts)),
        out_shape=(
            jax.ShapeDtypeStruct((latents + 16, total_rows), jnp.bfloat16),
            jax.ShapeDtypeStruct((latents, 1), jnp.float32),
            jax.ShapeDtypeStruct((1, latents), jnp.float32),
        ),
        in_specs=[SMEM] + [VMEM] * (len(acts) + len(decs)),
        out_specs=(VMEM, VMEM, VMEM),
        compiler_params=params(SMALL_VMEM),
        cost_estimate=estimate(4 * latents * width, 2 * latents * width),
        name="side",
    )(order, *acts, *decs)


def decoder_tasks(base, row_scale, left_ref, scale_ref, dec_ref, err, dec_out, dec_grad_ref, recon_ref, sems, outs):
    latents, wide = dec_ref.shape

    def task(spot, at, step):
        cols = slice(at, at + step)

        def product():
            return jnp.dot(left_ref[...], err[:, cols], preferred_element_type=jnp.float32)

        def use(both):
            grad = both[:latents] + scale_ref[...] * dec_ref[:, cols].astype(jnp.float32)
            dec_out[:, cols] = grad.astype(jnp.bfloat16)
            recon_ref[:, cols] = both[latents : latents + recon_ref.shape[0]] * row_scale
            start = pl.multiple_of(base + at, 128)
            out = pltpu.make_async_copy(dec_out.at[:, cols], dec_grad_ref.at[:, pl.ds(start, step)], sems.at[spot])
            out.start()
            outs.append(out)

        return product, use

    return [task(spot, at, step) for spot, (at, step) in enumerate(chunks(wide))]


def piece_base(core, half, side_index, offset):
    return jnp.where(core == side_index, 0, half) + offset


def grad_kernel(later, side_index, offset, half, row_scale, left_ref, scale_ref, dec_ref, *refs):
    blocks, refs = refs[:4], refs[4:]
    before, refs = (refs[0], refs[2:]) if later else (None, refs)
    total_ref, recon_ref, dec_grad_ref, dec_out, sems = refs
    base = piece_base(lax.axis_index("c"), half, side_index, offset)
    err = stack(blocks)
    outs = []

    def product():
        return lax.dot_general(err, dec_ref[...], (((1,), (1,)), ((), ())), preferred_element_type=jnp.float32)

    def use(result):
        total_ref[...] = before[...] + result if later else result

    pipelined(
        decoder_tasks(base, row_scale, left_ref, scale_ref, dec_ref, err, dec_out, dec_grad_ref, recon_ref, sems, outs)
        + [(product, use)]
    )
    for out in outs:
        out.wait()


def grad(left, scale, dec, blocks, held, side_index, offset, half, row_scale, out_rows):
    rows, wide = blocks[0].shape
    latents = dec.shape[0]
    later = held is not None
    return pl.pallas_call(
        functools.partial(grad_kernel, later, side_index, offset, half, row_scale),
        out_shape=(
            jax.ShapeDtypeStruct((4 * rows, latents), jnp.float32),
            jax.ShapeDtypeStruct((out_rows, wide), jnp.float32),
            jax.ShapeDtypeStruct((latents, 2 * half), jnp.bfloat16),
        ),
        in_specs=[VMEM] * 7 + ([VMEM, HBM] if later else []),
        out_specs=(VMEM, VMEM, HBM),
        scratch_shapes=[
            pltpu.VMEM((latents, wide), jnp.bfloat16),
            pltpu.SemaphoreType.DMA((len(chunks(wide)),)),
        ],
        input_output_aliases={8: 2} if later else {},
        compiler_params=params(SMALL_VMEM),
        cost_estimate=estimate(16 * rows * latents * wide, 4 * latents * wide),
        name="grad",
    )(left, scale, dec, *blocks, *(held if later else ()))


def tail_kernel(widths, row_scale, groups, left_ref, scale_ref, norm_ref, total_ref, dec_ref, *refs):
    count = len(widths)
    preacts, refs = refs[:groups], refs[groups:]
    recons, refs = refs[: 2 * count - 1], refs[2 * count - 1 :]
    e_blocks, refs = refs[:4], refs[4:]
    x_blocks, refs = [refs[4 * k : 4 * k + 4] for k in range(2 * count)], refs[8 * count + 1 :]
    dec_grad_ref, enc_grad_ref, bias_ref, recon_ref = refs[:4]
    dec_out, enc_out, recon_last, pre_ref, dec_sems, enc_sems = refs[4:]
    core = lax.axis_index("c")
    half = sum(widths)
    bases = []
    for k in range(2 * count):
        side_index, q = divmod(k, count)
        bases.append(piece_base(core, half, side_index, sum(widths[:q])))
    err = stack(e_blocks)
    outs = []

    def product():
        return lax.dot_general(err, dec_ref[...], (((1,), (1,)), ((), ())), preferred_element_type=jnp.float32)

    def use(result):
        act_grad = total_ref[...] + result + norm_ref[...]
        rounded = jnp.where(stack(preacts) > 0.0, act_grad, 0.0).astype(jnp.bfloat16)
        pre_ref[...] = rounded
        bias_ref[...] = jnp.sum(rounded.astype(jnp.float32), axis=0, keepdims=True)

    def encoder_task(spot, row, k, at, step):
        def product():
            mine = jnp.concatenate([ref[:, at : at + step] for ref in x_blocks[k]], axis=0)
            return lax.dot_general(mine, pre_ref[...], (((0,), (0,)), ((), ())), preferred_element_type=jnp.float32)

        def use(piece):
            enc_out[row : row + step] = piece.astype(jnp.bfloat16)
            start = pl.multiple_of(bases[k] + at, 128)
            out = pltpu.make_async_copy(
                enc_out.at[pl.ds(row, step), :], enc_grad_ref.at[pl.ds(start, step), :], enc_sems.at[spot]
            )
            out.start()
            outs.append(out)

        return product, use

    decoder = decoder_tasks(
        bases[-1], row_scale, left_ref, scale_ref, dec_ref, err, dec_out, dec_grad_ref, recon_last, dec_sems, outs
    )
    encoder = []
    row = 0
    for k in range(2 * count):
        for at, step in chunks(widths[k % count]):
            encoder.append(encoder_task(len(encoder), row, k, at, step))
            row += step
    tasks = [decoder.pop(0), (product, use), decoder.pop(0)]
    for spot, task in enumerate(encoder):
        tasks.append(task)
        if decoder and spot % 2 == 1:
            tasks.append(decoder.pop(0))
    pipelined(tasks)
    for k, held in enumerate(list(recons) + [recon_last]):
        recon_ref[:, pl.ds(pl.multiple_of(bases[k], 128), widths[k % count])] = held[...]
    for out in outs:
        out.wait()


def tail(left, preacts, scale, norm, total, dec, recons, e_blocks, x_blocks, dec_grad, row_scale, widths):
    rows = e_blocks[0].shape[0]
    latents = dec.shape[0]
    half = sum(widths)
    out_rows = recons[0].shape[0]
    spots = 2 * sum(len(chunks(w)) for w in widths)
    vmem_args = [left, scale, norm, total, dec, *preacts, *recons, *e_blocks, *[b for blocks in x_blocks for b in blocks]]
    return pl.pallas_call(
        functools.partial(tail_kernel, widths, row_scale, len(preacts)),
        out_shape=(
            jax.ShapeDtypeStruct((latents, 2 * half), jnp.bfloat16),
            jax.ShapeDtypeStruct((2 * half, latents), jnp.bfloat16),
            jax.ShapeDtypeStruct((1, latents), jnp.float32),
            jax.ShapeDtypeStruct((out_rows, 2 * half), jnp.float32),
        ),
        in_specs=[VMEM] * len(vmem_args) + [HBM],
        out_specs=(HBM, HBM, VMEM, VMEM),
        scratch_shapes=[
            pltpu.VMEM((latents, widths[-1]), jnp.bfloat16),
            pltpu.VMEM((2 * half, latents), jnp.bfloat16),
            pltpu.VMEM((out_rows, widths[-1]), jnp.float32),
            pltpu.VMEM((4 * rows, latents), jnp.bfloat16),
            pltpu.SemaphoreType.DMA((len(chunks(widths[-1])),)),
            pltpu.SemaphoreType.DMA((spots,)),
        ],
        input_output_aliases={len(vmem_args): 0},
        compiler_params=params(TAIL_VMEM),
        cost_estimate=estimate(24 * rows * latents * half, 8 * latents * half),
        name="tail",
    )(*vmem_args, dec_grad)


def per_device(tokens, batch_order, enc_weight, enc_bias, dec_weight):
    rows_dev, width = tokens.shape
    total_rows = batch_order.shape[0]
    row_scale = math.sqrt(total_rows)
    half = width // 2
    widths = (half,)
    block_rows = total_rows // 4
    core = lax.axis_index("c")

    got = swap_cores(tokens)
    low = jnp.concatenate([tokens[:, :half], got[:, :half]])
    high = jnp.concatenate([got[:, half:], tokens[:, half:]])
    block = jnp.where(core == 0, low, high)
    near = near_copies(block)
    x_own = spread(near)
    encs, decs = load(near, enc_weight, dec_weight, widths)
    done = []

    def work(group):
        oth = [swap_cores(x_own[k]) for k in group]
        pre_part, act, sibling = front([x_own[k] for k in group], oth, encs, enc_bias, decs[1])
        own = parts(act, decs[0], len(group))
        done.append((oth, pre_part, act, sibling, own))

    work(GROUPS[0])
    x_own[1:], encs, decs, done[0] = lax.optimization_barrier((x_own[1:], encs, decs, done[0]))
    for group in GROUPS[1:]:
        work(group)
    preacts, acts = [item[1] for item in done], [item[2] for item in done]
    x_oth, parts_oth, parts_own = [[a for item in done for a in item[k]] for k in (0, 3, 4)]
    got = [swap_cores(part) for part in parts_oth]
    total = parts_own[0].astype(jnp.float32) + got[0].astype(jnp.float32)
    for k in range(1, 4):
        sent = (parts_own[k].astype(jnp.float32) + got[k].astype(jnp.float32)).astype(jnp.bfloat16)
        total = total + lax.ppermute(sent, NAMES, SHIFTS[k - 1]).astype(jnp.float32)
    left, scale, norm = side(batch_order, acts, decs, row_scale, rows_dev)
    total = total.astype(jnp.bfloat16).reshape(16, block_rows // 16, half)
    total, left, scale, norm = lax.optimization_barrier((total, left, scale, norm))
    pieces = lax.all_to_all(total, CHIPS, 0, 0, axis_index_groups=CLASSES)
    recon = jnp.sum(pieces.astype(jnp.float32), axis=0) - block.astype(jnp.float32)
    err_block = (recon / row_scale).astype(jnp.bfloat16)
    near = near_copies(err_block)
    e_own = spread(near)
    e_oth = [swap_cores(a) for a in e_own]
    act_part, recon_own, dec_grad = grad(left, scale, decs[0], e_own, None, 0, 0, half, row_scale, rows_dev)
    dec_grad, enc_grad, bias_grad, recon_error = tail(
        left, preacts, scale, norm, act_part, decs[1], [recon_own], e_oth, [x_own, x_oth], dec_grad, row_scale,
        widths,
    )
    return (recon_error, enc_grad, dec_grad, bias_grad[0])


def solution(mesh):
    split = Mesh(mesh.devices.reshape(4, 2, 2, 4, 2), NAMES)
    return jax.shard_map(
        per_device,
        mesh=split,
        in_specs=(P(NAMES, None), P(), P(None, NAMES), P(NAMES), P(NAMES, None)),
        out_specs=(P(NAMES, None), P(None, NAMES), P(NAMES, None), P(NAMES)),
        check_vma=False,
    )
```
